32 devices in a mesh: dp: 4 (over y, core), seq: 8 (over z, x).
Axes of the slice: x: 2, y: 2, z: 4, core: 2. Of those that a mesh axis runs over, the one named last changes fastest.
Arguments:
- x_in: bfloat16 [4, 2048, 2048], P('dp', 'seq'), may hold values from -0.37 to 0.37
- b_in: bfloat16 [4, 2048, 128], P('dp', 'seq'), may hold values from -7.4 to 7.4
- c_in: bfloat16 [4, 2048, 128], P('dp', 'seq'), may hold values from -0.12988281 to 0.12988281
- dt: float32 [4, 32, 2048], P('dp', None, 'seq'), may hold values from 0.2 to 8192, as said below
- a_log: float32 [32], replicated, may hold values from -14 to -2, as said below
- skip: float32 [32], replicated, may hold values from 1 to 3
- cotangent: bfloat16 [4, 2048, 2048], P('dp', 'seq'), may hold values from -0.29882812 to 0.29882812
Outputs:
- y_out: bfloat16 [4, 2048, 2048], P('dp', 'seq')
- grad_x: bfloat16 [4, 2048, 2048], P('dp', 'seq')
- grad_b: bfloat16 [4, 2048, 128], P('dp', 'seq')
- grad_c: bfloat16 [4, 2048, 128], P('dp', 'seq')
- grad_dt: float32 [4, 32, 2048], P('dp', None, 'seq')
- grad_alog: float32 [32], replicated
- derivative_bypass: float32 [32], replicated
The draws below stay inside these ranges and needn't reach their ends.
Inputs may be any that keep to these rules, and one draw needn't show every extreme that they name: `dt`: positive step sizes. Each head's decay rate exp(a_log) is positive.
All inputs are finite; a program needn't handle non-finite values.
Results may differ from the reference program's by a relative error of at most 0.018.
Values sent between devices are 32-bit elements; how exact they have to be, the bound alone decides.
A program may use at most 128 MiB of HBM per device.

```python
import jax
import jax.numpy as jnp
from jax import lax

H = 32
P_SIZE = 64
N = 128
GROUP = 256
TOK_DEV = 256
SEQLEN = 2048
BATCH = 4
HP = 2048


def decay_rates(key):
    base_key = jax.random.fold_in(key, 11)
    pick_key, slow_key, fast_key = jax.random.split(base_key, 3)
    slow_share = 0.5
    slow_mask = jax.random.uniform(pick_key, (H,), jnp.float32) < slow_share
    slow_rate = jax.random.uniform(slow_key, (H,), jnp.float32, 0.2, 0.8) / SEQLEN
    fast_rate = jnp.exp(jax.random.uniform(fast_key, (H,), jnp.float32, -1.204, 0.0)) / TOK_DEV
    return jnp.where(slow_mask, slow_rate, fast_rate)


def device_levels(key):
    level_key = jax.random.fold_in(key, 37)
    return jnp.exp(jax.random.uniform(level_key, (BATCH, SEQLEN // TOK_DEV, 1, 1), jnp.float32, -2.5, 0.2))


def loud_field(key, offset_number, width, spread):
    field_key = jax.random.fold_in(key, offset_number)
    field_shape = (BATCH, SEQLEN // TOK_DEV, TOK_DEV, width)
    entries = jax.random.truncated_normal(field_key, -6.0, 6.0, field_shape, jnp.float32)
    shaped = entries * spread * device_levels(key)
    return shaped.reshape(BATCH, SEQLEN, width).astype(jnp.bfloat16)


def draw_x_in(key, part):
    return loud_field(key, 41, HP, 0.05)


def draw_b_in(key, part):
    return loud_field(key, 43, N, 1.0)


def draw_a_log(key, part):
    return jnp.log(decay_rates(key))


def draw_dt(key, part):
    speed_numbers = decay_rates(key)
    step_key = jax.random.fold_in(key, 23)
    rough_key, plateau_key, spot_key, loss_key = jax.random.split(step_key, 4)
    roughness = jnp.exp(jax.random.uniform(rough_key, (BATCH, H, SEQLEN), jnp.float32, -0.693, 0.693))
    level_count = SEQLEN // TOK_DEV
    plateau = jnp.exp(jax.random.uniform(plateau_key, (BATCH, 1, level_count, 1), jnp.float32, -0.7, 0.7))
    plateau = jnp.broadcast_to(plateau, (BATCH, H, level_count, TOK_DEV)).reshape(BATCH, H, SEQLEN)
    point_offsets = jax.random.randint(spot_key, (BATCH, 2), 0, SEQLEN)
    objective_numbers = jax.random.uniform(loss_key, (BATCH, 2), jnp.float32, 0.22, 0.69)
    location_numbers = jnp.arange(SEQLEN)[None, :]
    segment_extent = jnp.where(location_numbers == point_offsets[:, 0:1], objective_numbers[:, 0:1], jnp.where(location_numbers == point_offsets[:, 1:2], objective_numbers[:, 1:2], 0.0))
    equilibrium_memory = roughness * plateau
    return jnp.where(segment_extent[:, None, :] > 0.0, segment_extent[:, None, :] / speed_numbers[None, :, None], equilibrium_memory)


def steps_of(own_key, extent, cuts, low, top_value):
    def one(position, blocks):
        heights = jax.random.uniform(jax.random.fold_in(jax.random.fold_in(own_key, 6), position), (blocks,), jnp.float32, low / len(cuts), top_value / len(cuts))
        return jnp.repeat(jnp.exp(heights), extent[position] // blocks).reshape((-1,) + (1,) * (len(extent) - position - 1))

    factor_of = one(*cuts[0])
    for cut in cuts[1:]:
        factor_of = factor_of * one(*cut)
    return factor_of


def noise(key, dims, deviation, limit, pieces=(), kind=jnp.bfloat16):
    level = steps_of(key, dims, pieces, -0.22, 0.18) if pieces else 1.0
    values = jax.random.normal(key, dims, jnp.float32) * deviation * level
    return jnp.minimum(jnp.maximum(values, -limit), limit).astype(kind)


def setup_inputs(seed: int = 0) -> dict:
    streams_of = jax.random.split(jax.random.key(seed), 8)
    return {
        "x_in": draw_x_in(jax.random.fold_in(streams_of[7], 71), 0),
        "b_in": draw_b_in(jax.random.fold_in(streams_of[7], 71), 0),
        "c_in": noise(streams_of[2], (BATCH, SEQLEN, N), 0.022, 0.12988281, ((0, 4), (1, 8))),
        "dt": draw_dt(jax.random.fold_in(streams_of[7], 71), 0),
        "a_log": draw_a_log(jax.random.fold_in(streams_of[7], 71), 0),
        "skip": jnp.clip(jax.random.uniform(streams_of[5], (H,), jnp.float32, 1.0, 3.0), 1.0, 3.0),
        "cotangent": noise(streams_of[6], (BATCH, SEQLEN, HP), 0.05, 0.29882812, ((0, 4), (1, 8))),
    }


def piece_state(x_block, b_block, log_decay):
    span = x_block.shape[0]
    head_count = log_decay.shape[0]
    feat_width = x_block.shape[1]
    head_size = feat_width // head_count
    cum_log = jnp.cumsum(log_decay, axis=1)
    to_end = jnp.exp(cum_log[:, -1:] - cum_log)
    scaled = (x_block.reshape(span, head_count, head_size).astype(jnp.float32) * to_end.T[:, :, None]).astype(jnp.bfloat16)
    block_state = lax.dot_general(scaled.reshape(span, feat_width), b_block, (((0,), (0,)), ((), ())), preferred_element_type=jnp.float32)
    return (jnp.exp(cum_log[:, -1]), block_state.reshape(head_count, head_size, b_block.shape[1]))

def piece_out(x_block, b_block, c_block, log_decay, skip_gain, state_in):
    span = x_block.shape[0]
    head_count = log_decay.shape[0]
    feat_width = x_block.shape[1]
    head_size = feat_width // head_count
    cum_log = jnp.cumsum(log_decay, axis=1)
    inner_cb = jnp.dot(c_block, b_block.T, preferred_element_type=jnp.float32)
    row_ids = lax.broadcasted_iota(jnp.int32, (span, span), 0)
    col_ids = lax.broadcasted_iota(jnp.int32, (span, span), 1)
    lower = (row_ids >= col_ids)[None]
    differ = jnp.where(lower, cum_log[:, :, None] - cum_log[:, None, :], 0.0)
    weights = jnp.where(lower, inner_cb[None] * jnp.exp(differ), 0.0).astype(jnp.bfloat16)
    x_heads = x_block.reshape(span, head_count, head_size)
    inner = jnp.einsum('htu,uhp->thp', weights.astype(jnp.float32), x_heads.astype(jnp.float32))
    state_low = state_in.astype(jnp.bfloat16)
    carried = jnp.einsum('tn,hpn->thp', c_block.astype(jnp.float32), state_low.astype(jnp.float32))
    carried = carried * jnp.exp(cum_log).T[:, :, None]
    result = inner + carried + skip_gain[None, :, None] * x_heads.astype(jnp.float32)
    return result.reshape(span, feat_width)

def reference(x_in, b_in, c_in, dt, a_log, skip, cotangent):
    block_count = SEQLEN // GROUP

    def forward(x_all, b_all, c_all, dt_all, a_param, skip_param):
        la_all = -jnp.exp(a_param)[None, :, None] * dt_all

        def one_sequence(fragments):
            x_seq, b_seq, c_seq, la_seq = fragments
            x_blocks = x_seq.reshape(block_count, GROUP, H * P_SIZE)
            b_blocks = b_seq.reshape(block_count, GROUP, N)
            c_blocks = c_seq.reshape(block_count, GROUP, N)
            la_blocks = la_seq.reshape(H, block_count, GROUP).transpose(1, 0, 2)

            def advance(state_now, piece):
                x_block, b_block, c_block, log_decay = piece
                y_block = piece_out(x_block, b_block, c_block, log_decay, skip_param, state_now)
                gain, block_state = piece_state(x_block, b_block, log_decay)
                return (gain[:, None, None] * state_now + block_state, y_block)
            start = jnp.zeros((H, P_SIZE, N), jnp.float32)
            _, outputs = lax.scan(jax.checkpoint(advance), start, (x_blocks, b_blocks, c_blocks, la_blocks))
            return outputs.reshape(SEQLEN, H * P_SIZE)
        return lax.map(one_sequence, (x_all, b_all, c_all, la_all))
    y_full, pull_back = jax.vjp(forward, x_in, b_in, c_in, dt, a_log, skip)
    grad_x, grad_b, grad_c, grad_dt, grad_alog, derivative_bypass = pull_back(cotangent.astype(jnp.float32))
    return (y_full.astype(jnp.bfloat16), grad_x, grad_b, grad_c, grad_dt, grad_alog, derivative_bypass)
```

```python
import functools

import jax
import jax.numpy as jnp
from jax import lax
from jax.experimental import pallas as pl
from jax.experimental.pallas import tpu as pltpu
from jax.sharding import PartitionSpec as P

F32 = jnp.float32
BF16 = jnp.bfloat16
MESH = pl.DeviceIdType.MESH
LANES = 128


def dot(a, b, ca=1, cb=0, precision=None):
    return lax.dot_general(
        a, b, (((ca,), (cb,)), ((), ())), preferred_element_type=F32, precision=precision
    )


def pack(v, heads):
    lane = lax.broadcasted_iota(jnp.int32, v.shape, 1)
    hi = v.astype(BF16).astype(F32)
    rest = v - hi
    mid = rest.astype(BF16).astype(F32)
    low = rest - mid
    out = jnp.where(lane < heads, hi, jnp.where(lane < 2 * heads, mid, low))
    return jnp.where(lane < 3 * heads, out, 0.0).astype(BF16)


def halves(v):
    hi = v.astype(BF16)
    return hi, (v - hi.astype(F32)).astype(BF16)


def kernel(
    n_seq,
    n_dp,
    width,
    x_ref,
    b_ref,
    c_ref,
    dt_ref,
    alog_ref,
    skip_ref,
    g_ref,
    y_ref,
    gx_ref,
    gb_ref,
    gc_ref,
    gdt_ref,
    ga_ref,
    gs_ref,
    spread,
    cum_rows,
    cum_pack,
    e_wide,
    to_wide,
    scaled,
    dv,
    bt,
    ct,
    local,
    p_in,
    p_out,
    m_in,
    m_out,
    rows,
    y_acc,
    dx_acc,
    cb_ref,
    dcb,
    dc_acc,
    db_acc,
    dcum,
    gain_own,
    gain_in,
    red_seq,
    red_dp,
    p_send,
    p_recv,
    m_send,
    m_recv,
    g_sem,
    rs_send,
    rs_recv,
    rd_send,
    rd_recv,
):
    heads, span = dt_ref.shape
    feat = x_ref.shape[1]
    size = feat // heads
    chunks = feat // width
    pairs = n_seq // 2
    me = lax.axis_index("seq")
    mine = lax.axis_index("dp")
    place = me // 2
    odd = lax.rem(me, 2)
    partner = me + 1 - 2 * odd

    barrier = pltpu.get_barrier_semaphore()

    def greet_seq(o, carry):
        pl.semaphore_signal(
            barrier, inc=1, device_id={"seq": lax.rem(me + o, n_seq)}, device_id_type=MESH
        )
        return carry

    def greet_dp(o, carry):
        pl.semaphore_signal(
            barrier, inc=1, device_id={"dp": lax.rem(mine + o, n_dp)}, device_id_type=MESH
        )
        return carry

    lax.fori_loop(1, n_seq, greet_seq, 0)
    lax.fori_loop(1, n_dp, greet_dp, 0)

    diag = lax.broadcasted_iota(jnp.int32, (heads, heads), 0) == lax.broadcasted_iota(
        jnp.int32, (heads, heads), 1
    )

    def column(row):
        return jnp.sum(jnp.where(diag, jnp.broadcast_to(row, (heads, heads)), 0.0), 1, keepdims=True)

    def as_row(col):
        return jnp.sum(jnp.where(diag, jnp.broadcast_to(col, (heads, heads)), 0.0), 0, keepdims=True)

    rate = jnp.exp(column(alog_ref[...]))
    la = -rate * dt_ref[...]
    t_row = lax.broadcasted_iota(jnp.int32, (span, span), 0)
    t_col = lax.broadcasted_iota(jnp.int32, (span, span), 1)
    upper = jnp.where(t_row <= t_col, 1.0, 0.0).astype(F32)
    cum = dot(jnp.concatenate([la] * (LANES // heads), 0), upper, precision=lax.Precision.HIGHEST)
    cum_rows[...] = cum
    cum_t = jnp.transpose(cum)
    cum_pack[...] = pack(cum_t, heads)
    e_t = jnp.exp(cum_t)
    gain_own[...] = e_t[span - 16 :, :]
    pl.semaphore_wait(barrier, n_seq - 1 + n_dp - 1)
    gain_copy = pltpu.make_async_remote_copy(
        src_ref=gain_own,
        dst_ref=gain_in,
        send_sem=g_sem.at[0],
        recv_sem=g_sem.at[1],
        device_id={"seq": partner},
        device_id_type=MESH,
    )
    gain_copy.start()

    e_pack = pack(e_t, heads)
    to_pack = pack(jnp.exp(cum_t[span - 1 :, :] - cum_t), heads)
    spread_row = lax.rem(lax.broadcasted_iota(jnp.int32, spread.shape, 0), heads)
    spread_col = lax.broadcasted_iota(jnp.int32, spread.shape, 1) // size
    spread[...] = jnp.where(spread_row == spread_col, 1.0, 0.0).astype(BF16)
    bt[...] = jnp.transpose(b_ref[...].astype(F32)).astype(BF16)
    ct[...] = jnp.transpose(c_ref[...].astype(F32)).astype(BF16)
    skip_col = jnp.broadcast_to(column(skip_ref[...]), (heads, LANES))
    skip_pack = pack(jnp.transpose(jnp.concatenate([skip_col] * (LANES // heads), 0)), heads)

    def part(c):
        return pl.ds(pl.multiple_of(c * width, width), width)

    def prepare(c, carry):
        cols = part(c)
        spread_c = spread[:, cols]
        e_c = dot(e_pack, spread_c)
        to_c = dot(to_pack, spread_c)
        e_wide[:, cols] = e_c
        to_wide[:, cols] = to_c
        x_c = x_ref[:, cols].astype(F32)
        g_c = g_ref[:, cols].astype(F32)
        sc = (x_c * to_c).astype(BF16)
        dv_c = (g_c * e_c).astype(BF16)
        scaled[:, cols] = sc
        dv[:, cols] = dv_c
        local[0, c] = dot(bt[...], sc)
        local[1, c] = dot(ct[...], dv_c)
        rows[0:1, cols] = e_c[span - 1 :, :]
        rows[2:3, cols] = dot(skip_pack[0:16], spread_c)[0:1]
        rows[4:5, cols] = jnp.sum(x_c * g_c, 0, keepdims=True)
        return carry

    lax.fori_loop(0, chunks, prepare, 0)

    gain_copy.wait()
    gain_pack = pack(gain_in[...], heads)
    rows[1:2, :] = dot(gain_pack, spread[...])[15:16, :]

    def role(d):
        lead = odd == d
        steps = jnp.where(d == 0, place, pairs - 1 - place)
        lead_row = jnp.broadcast_to(jnp.where(lead, 1, 0), (1, width)) == 1
        return lead, steps, lead_row

    def p_copy(d, c):
        return pltpu.make_async_remote_copy(
            src_ref=p_out.at[d, c],
            dst_ref=p_in.at[d, c],
            send_sem=p_send.at[d, c],
            recv_sem=p_recv.at[d, c],
            device_id={"seq": lax.rem(me + 2 - 4 * d + n_seq, n_seq)},
            device_id_type=MESH,
        )

    def m_copy(d, c):
        return pltpu.make_async_remote_copy(
            src_ref=m_out.at[d, c],
            dst_ref=m_in.at[d, c],
            send_sem=m_send.at[d, c],
            recv_sem=m_recv.at[d, c],
            device_id={"seq": partner},
            device_id_type=MESH,
        )

    def step(d, c, at_start):
        lead, steps, lead_row = role(d)
        cols = part(c)
        own = rows[0:1, cols]
        other = rows[1:2, cols]
        here = local[d, c]
        if at_start:
            p_in[d, c] = jnp.zeros_like(here)

            @pl.when(lead)
            def _():
                m_out[d, c] = here
                m_copy(d, c).start()

            p_out[d, c] = jnp.where(lead_row, other, 1.0) * here
            p_copy(d, c).start()
        else:
            p_copy(d, c).wait_recv()
            before = p_in[d, c]

            @pl.when(steps < pairs - 1)
            def _():
                p_out[d, c] = own * other * before + jnp.where(lead_row, other, 1.0) * here
                p_copy(d, c).start()

            m_out[d, c] = jnp.where(lead_row, own, 1.0) * before + jnp.where(lead_row, here, 0.0)
            m_copy(d, c).start()

    def begin(c, carry):
        @pl.when(place == 0)
        def _():
            step(0, c, True)

        @pl.when(place == pairs - 1)
        def _():
            step(1, c, True)

        return carry

    lax.fori_loop(0, chunks, begin, 0)

    cb_ref[...] = dot(c_ref[...], b_ref[...], 1, 1)
    dcb[...] = jnp.zeros_like(dcb)

    def inner(j, carry):
        cols = pl.ds(pl.multiple_of(j * 2 * size, 2 * size), 2 * size)
        x2 = x_ref[:, cols]
        g2 = g_ref[:, cols]
        lane = lax.broadcasted_iota(jnp.int32, (span, 2 * size), 1)
        lower = t_row >= t_col
        y2, dx2 = [], []
        total = dcb[...]
        for i in range(2):
            h = 2 * j + i
            pick_row = lax.broadcasted_iota(jnp.int32, (LANES, span), 0)
            pick = jnp.where(lax.rem(pick_row, heads) == h, 1.0, 0.0).astype(BF16)
            at_t = dot(cum_pack[...], pick)
            decay = jnp.exp(jnp.where(lower, at_t - cum_rows[pl.ds(h, 1), :], -1e30))
            weights = (cb_ref[...] * decay).astype(BF16)
            y2.append(dot(weights, x2))
            dx2.append(dot(weights, g2, 0, 0))
            own_lanes = (lane < size) if i == 0 else (lane >= size)
            g_own = jnp.where(own_lanes, g2.astype(F32), 0.0).astype(BF16)
            total = total + dot(g_own, x2, 1, 1) * decay
        dcb[...] = total
        y_acc[:, cols] = jnp.where(lane < size, y2[0], y2[1])
        dx_acc[:, cols] = jnp.where(lane < size, dx2[0], dx2[1])
        return carry

    per_chunk = width // (2 * size)
    upper_half = jnp.where(place >= pairs // 2, 1, 0)

    def middle(c, carry):
        for s in range(2):
            d = upper_half + s - 2 * s * upper_half
            _, steps, _ = role(d)

            @pl.when(steps > 0)
            def _():
                step(d, c, False)

        return lax.fori_loop(c * per_chunk, (c + 1) * per_chunk, inner, carry)

    lax.fori_loop(0, chunks, middle, 0)

    dcb_low = dcb[...]
    dc_acc[...] = dot(dcb_low.astype(BF16), b_ref[...])
    db_acc[...] = dot(jnp.transpose(dcb_low).astype(BF16), c_ref[...])
    dcum[...] = jnp.zeros_like(dcum)

    def entering(d, c):
        lead, steps, lead_row = role(d)
        nothing = jnp.logical_and(lead, steps == 0)

        @pl.when(nothing)
        def _():
            m_in[d, c] = jnp.zeros((LANES, width), F32)

        @pl.when(jnp.logical_not(nothing))
        def _():
            m_copy(d, c).wait_recv()

        factor = jnp.where(lead_row, 1.0, rows[1:2, part(c)])
        return factor * p_in[d, c] + m_in[d, c]

    def finish(c, carry):
        cols = part(c)
        state = entering(0, c)
        adj = entering(1, c)
        state_low = state.astype(BF16)
        adj_low = adj.astype(BF16)
        x_c = x_ref[:, cols].astype(F32)
        g_c = g_ref[:, cols].astype(F32)
        skip_c = rows[2:3, cols]
        y_c = y_acc[:, cols] + e_wide[:, cols] * dot(c_ref[...], state_low)
        y_ref[:, cols] = (y_c + skip_c * x_c).astype(BF16)
        dx_state = to_wide[:, cols] * dot(b_ref[...], adj_low)
        dx_c = dx_acc[:, cols] + dx_state
        gx_ref[:, cols] = (dx_c + skip_c * g_c).astype(BF16)
        dc_acc[...] += dot(dv[:, cols], state_low, 1, 1)
        db_acc[...] += dot(scaled[:, cols], adj_low, 1, 1)
        hi, low = halves(g_c * y_c - x_c * dx_c)
        sel = spread[0:heads, cols]
        dcum[...] += dot(sel, hi, 1, 1) + dot(sel, low, 1, 1)
        rows[3:4, cols] = jnp.sum(x_c * dx_state, 0, keepdims=True) + rows[0:1, cols] * jnp.sum(
            state * adj, 0, keepdims=True
        )
        return carry

    lax.fori_loop(0, chunks, finish, 0)

    sums = jnp.concatenate([rows[3:5, :], jnp.zeros((14, feat), F32)], 0)
    hi, low = halves(sums)
    sel = spread[0:heads, :]
    per_head = dot(sel, hi, 1, 1) + dot(sel, low, 1, 1)
    lower_f = jnp.where(t_row >= t_col, 1.0, 0.0).astype(F32)
    dla = dot(dcum[...], lower_f, precision=lax.Precision.HIGHEST) + per_head[:, 0:1]
    gdt_ref[...] = -rate * dla
    alog_row = as_row(jnp.sum(dla * la, 1, keepdims=True))
    skip_row = as_row(per_head[:, 1:2])

    red_seq[me] = jnp.zeros((8, LANES), F32)
    red_seq[me, 0:1, 0:heads] = alog_row
    red_seq[me, 1:2, 0:heads] = skip_row

    def share(axis, here, count, buf, send, recv):
        def copy(target, slot, o):
            return pltpu.make_async_remote_copy(
                src_ref=buf.at[here],
                dst_ref=buf.at[slot],
                send_sem=send.at[o],
                recv_sem=recv.at[slot],
                device_id={axis: target},
                device_id_type=MESH,
            )

        def go(o, carry):
            copy(lax.rem(here + o, count), here, o).start()
            return carry

        def come(o, carry):
            source = lax.rem(here + o, count)
            copy(source, source, o).wait_recv()
            copy(source, here, o).wait_send()
            return carry

        lax.fori_loop(1, count, go, 0)
        lax.fori_loop(1, count, come, 0)
        return jnp.sum(buf[...], 0)

    red_dp[mine] = share("seq", me, n_seq, red_seq, rs_send, rs_recv)
    total = share("dp", mine, n_dp, red_dp, rd_send, rd_recv)
    ga_ref[...] = total[0:1, 0:heads]
    gs_ref[...] = total[1:2, 0:heads]
    gc_ref[...] = dc_acc[...].astype(BF16)
    gb_ref[...] = db_acc[...].astype(BF16)

    def drain(c, carry):
        for d in range(2):
            lead, steps, _ = role(d)

            @pl.when(steps < pairs - 1)
            def _():
                p_copy(d, c).wait_send()

            @pl.when(jnp.logical_or(lead, steps > 0))
            def _():
                m_copy(d, c).wait_send()

        return carry

    lax.fori_loop(0, chunks, drain, 0)


def shards(n_seq, n_dp, x_in, b_in, c_in, dt, a_log, skip, cotangent):
    _, span, feat = x_in.shape
    state_dim = b_in.shape[2]
    heads = a_log.shape[0]
    width = 256
    chunks = feat // width
    blocks = (2, chunks, state_dim, width)
    vmem = pl.BlockSpec(memory_space=pltpu.VMEM)
    dma = pltpu.SemaphoreType.DMA
    wide = pltpu.VMEM((span, feat), F32)
    wide_low = pltpu.VMEM((span, feat), BF16)
    outs = pl.pallas_call(
        functools.partial(kernel, n_seq, n_dp, width),
        out_shape=(
            jax.ShapeDtypeStruct((span, feat), BF16),
            jax.ShapeDtypeStruct((span, feat), BF16),
            jax.ShapeDtypeStruct((span, state_dim), BF16),
            jax.ShapeDtypeStruct((span, state_dim), BF16),
            jax.ShapeDtypeStruct((heads, span), F32),
            jax.ShapeDtypeStruct((1, heads), F32),
            jax.ShapeDtypeStruct((1, heads), F32),
        ),
        in_specs=[vmem] * 7,
        out_specs=(vmem,) * 7,
        scratch_shapes=[
            pltpu.VMEM((LANES, feat), BF16),
            pltpu.VMEM((LANES, span), F32),
            pltpu.VMEM((span, LANES), BF16),
            wide,
            wide,
            wide_low,
            wide_low,
            pltpu.VMEM((state_dim, span), BF16),
            pltpu.VMEM((state_dim, span), BF16),
            pltpu.VMEM(blocks, F32),
            pltpu.VMEM(blocks, F32),
            pltpu.VMEM(blocks, F32),
            pltpu.VMEM(blocks, F32),
            pltpu.VMEM(blocks, F32),
            pltpu.VMEM((8, feat), F32),
            wide,
            wide,
            pltpu.VMEM((span, span), F32),
            pltpu.VMEM((span, span), F32),
            pltpu.VMEM((span, state_dim), F32),
            pltpu.VMEM((span, state_dim), F32),
            pltpu.VMEM((heads, span), F32),
            pltpu.VMEM((16, LANES), F32),
            pltpu.VMEM((16, LANES), F32),
            pltpu.VMEM((n_seq, 8, LANES), F32),
            pltpu.VMEM((n_dp, 8, LANES), F32),
            dma((2, chunks)),
            dma((2, chunks)),
            dma((2, chunks)),
            dma((2, chunks)),
            dma((2,)),
            dma((n_seq,)),
            dma((n_seq,)),
            dma((n_dp,)),
            dma((n_dp,)),
        ],
        compiler_params=pltpu.CompilerParams(
            collective_id=0, has_side_effects=True, vmem_limit_bytes=48 * 1024 * 1024
        ),
    )(x_in[0], b_in[0], c_in[0], dt[0], a_log[None], skip[None], cotangent[0])
    y, gx, gb, gc, gdt, ga, gs = outs
    return (y[None], gx[None], gb[None], gc[None], gdt[None], ga[0], gs[0])


def solution(mesh):
    tokens = P("dp", "seq", None)
    steps = P("dp", None, "seq")
    return jax.shard_map(
        functools.partial(shards, mesh.shape["seq"], mesh.shape["dp"]),
        mesh=mesh,
        in_specs=(tokens, tokens, tokens, steps, P(), P(), tokens),
        out_specs=(tokens, tokens, tokens, tokens, steps, P(), P()),
        check_vma=False,
    )
```

```python
import functools

import jax
import jax.numpy as jnp
from jax import lax
from jax.experimental import pallas as pl
from jax.experimental.pallas import tpu as pltpu
from jax.sharding import PartitionSpec as P

F32 = jnp.float32
BF16 = jnp.bfloat16
MESH = pl.DeviceIdType.MESH
LANES = 128
VMEM_BYTES = 62 * 1024 * 1024


def dot(a, b, ca=1, cb=0, precision=None):
    return lax.dot_general(
        a, b, (((ca,), (cb,)), ((), ())), preferred_element_type=F32, precision=precision
    )


def pack(v, heads):
    lane = lax.broadcasted_iota(jnp.int32, v.shape, 1)
    hi = v.astype(BF16).astype(F32)
    rest = v - hi
    mid = rest.astype(BF16).astype(F32)
    low = rest - mid
    out = jnp.where(lane < heads, hi, jnp.where(lane < 2 * heads, mid, low))
    return jnp.where(lane < 3 * heads, out, 0.0).astype(BF16)


def halves(v):
    hi = v.astype(BF16)
    return hi, (v - hi.astype(F32)).astype(BF16)


def kernel(
    n_seq,
    n_dp,
    width,
    x_hbm,
    b_hbm,
    c_hbm,
    dt_hbm,
    alog_hbm,
    skip_hbm,
    g_hbm,
    y_hbm,
    gx_hbm,
    gb_hbm,
    gc_hbm,
    gdt_hbm,
    ga_ref,
    gs_ref,
    y_ref,
    gx_ref,
    gb_ref,
    gc_ref,
    gdt_ref,
    x_ref,
    b_ref,
    c_ref,
    dt_ref,
    alog_ref,
    skip_ref,
    g_ref,
    spread,
    cum_rows,
    cum_pack,
    e_wide,
    to_wide,
    scaled,
    dv,
    bt,
    ct,
    local,
    p_in,
    p_out,
    m_in,
    m_out,
    rows,
    y_acc,
    dx_acc,
    cb_ref,
    dcb,
    dc_acc,
    db_acc,
    dcum,
    gain_own,
    gain_in,
    red_seq,
    red_dp,
    p_send,
    p_recv,
    m_send,
    m_recv,
    g_sem,
    load_sem,
    store_sem,
    rs_send,
    rs_recv,
    rd_send,
    rd_recv,
):
    heads, span = dt_ref.shape
    feat = x_ref.shape[1]
    size = feat // heads
    chunks = feat // width
    pairs = n_seq // 2
    me = lax.axis_index("seq")
    mine = lax.axis_index("dp")
    place = me // 2
    odd = lax.rem(me, 2)
    partner = me + 1 - 2 * odd

    moves = [
        pltpu.make_async_copy(src, dst, load_sem.at[i])
        for i, (src, dst) in enumerate(
            [
                (dt_hbm, dt_ref),
                (alog_hbm, alog_ref),
                (skip_hbm, skip_ref),
                (b_hbm, b_ref),
                (c_hbm, c_ref),
                (x_hbm, x_ref),
                (g_hbm, g_ref),
            ]
        )
    ]
    for move in moves:
        move.start()
    barrier = pltpu.get_barrier_semaphore()

    def greet_seq(o, carry):
        pl.semaphore_signal(
            barrier, inc=1, device_id={"seq": lax.rem(me + o, n_seq)}, device_id_type=MESH
        )
        return carry

    def greet_dp(o, carry):
        pl.semaphore_signal(
            barrier, inc=1, device_id={"dp": lax.rem(mine + o, n_dp)}, device_id_type=MESH
        )
        return carry

    lax.fori_loop(1, n_seq, greet_seq, 0)
    lax.fori_loop(1, n_dp, greet_dp, 0)

    diag = lax.broadcasted_iota(jnp.int32, (heads, heads), 0) == lax.broadcasted_iota(
        jnp.int32, (heads, heads), 1
    )

    def column(row):
        return jnp.sum(jnp.where(diag, jnp.broadcast_to(row, (heads, heads)), 0.0), 1, keepdims=True)

    def as_row(col):
        return jnp.sum(jnp.where(diag, jnp.broadcast_to(col, (heads, heads)), 0.0), 0, keepdims=True)

    for move in moves[:3]:
        move.wait()
    rate = jnp.exp(column(alog_ref[...]))
    la = -rate * dt_ref[...]
    t_row = lax.broadcasted_iota(jnp.int32, (span, span), 0)
    t_col = lax.broadcasted_iota(jnp.int32, (span, span), 1)
    upper = jnp.where(t_row <= t_col, 1.0, 0.0).astype(F32)
    cum = dot(jnp.concatenate([la] * (LANES // heads), 0), upper, precision=lax.Precision.HIGHEST)
    cum_rows[...] = cum
    cum_t = jnp.transpose(cum)
    cum_pack[...] = pack(cum_t, heads)
    e_t = jnp.exp(cum_t)
    gain_own[...] = e_t[span - 16 :, :]
    pl.semaphore_wait(barrier, n_seq - 1 + n_dp - 1)
    gain_copy = pltpu.make_async_remote_copy(
        src_ref=gain_own,
        dst_ref=gain_in,
        send_sem=g_sem.at[0],
        recv_sem=g_sem.at[1],
        device_id={"seq": partner},
        device_id_type=MESH,
    )
    gain_copy.start()

    e_pack = pack(e_t, heads)
    to_pack = pack(jnp.exp(cum_t[span - 1 :, :] - cum_t), heads)
    spread_row = lax.rem(lax.broadcasted_iota(jnp.int32, spread.shape, 0), heads)
    spread_col = lax.broadcasted_iota(jnp.int32, spread.shape, 1) // size
    spread[...] = jnp.where(spread_row == spread_col, 1.0, 0.0).astype(BF16)
    for move in moves[3:]:
        move.wait()
    bt[...] = jnp.transpose(b_ref[...].astype(F32)).astype(BF16)
    ct[...] = jnp.transpose(c_ref[...].astype(F32)).astype(BF16)
    skip_col = jnp.broadcast_to(column(skip_ref[...]), (heads, LANES))
    skip_pack = pack(jnp.transpose(jnp.concatenate([skip_col] * (LANES // heads), 0)), heads)

    def part(c):
        return pl.ds(pl.multiple_of(c * width, width), width)

    cb_ref[...] = dot(c_ref[...], b_ref[...], 1, 1)
    dcb[...] = jnp.zeros_like(dcb)

    gain_copy.wait()
    gain_pack = pack(gain_in[...], heads)
    rows[1:2, :] = dot(gain_pack, spread[...])[15:16, :]

    def role(d):
        lead = odd == d
        steps = jnp.where(d == 0, place, pairs - 1 - place)
        lead_row = jnp.broadcast_to(jnp.where(lead, 1, 0), (1, width)) == 1
        return lead, steps, lead_row

    def p_copy(d, c):
        return pltpu.make_async_remote_copy(
            src_ref=p_out.at[d, c],
            dst_ref=p_in.at[d, c],
            send_sem=p_send.at[d, c],
            recv_sem=p_recv.at[d, c],
            device_id={"seq": lax.rem(me + 2 - 4 * d + n_seq, n_seq)},
            device_id_type=MESH,
        )

    def m_copy(d, c):
        return pltpu.make_async_remote_copy(
            src_ref=m_out.at[d, c],
            dst_ref=m_in.at[d, c],
            send_sem=m_send.at[d, c],
            recv_sem=m_recv.at[d, c],
            device_id={"seq": partner},
            device_id_type=MESH,
        )

    def step(d, c, at_start):
        lead, steps, lead_row = role(d)
        cols = part(c)
        own = rows[0:1, cols]
        other = rows[1:2, cols]
        here = local[d, c]
        if at_start:
            p_in[d, c] = jnp.zeros_like(here)

            @pl.when(lead)
            def _():
                m_out[d, c] = here
                m_copy(d, c).start()

            p_out[d, c] = jnp.where(lead_row, other, 1.0) * here
            p_copy(d, c).start()
        else:
            p_copy(d, c).wait_recv()
            before = p_in[d, c]

            @pl.when(steps < pairs - 1)
            def _():
                p_out[d, c] = own * other * before + jnp.where(lead_row, other, 1.0) * here
                p_copy(d, c).start()

            m_out[d, c] = jnp.where(lead_row, own, 1.0) * before + jnp.where(lead_row, here, 0.0)
            m_copy(d, c).start()

    def prepare(c, carry):
        cols = part(c)
        spread_c = spread[:, cols]
        e_c = dot(e_pack, spread_c)
        to_c = dot(to_pack, spread_c)
        e_wide[:, cols] = e_c
        to_wide[:, cols] = to_c
        x_c = x_ref[:, cols].astype(F32)
        g_c = g_ref[:, cols].astype(F32)
        sc = (x_c * to_c).astype(BF16)
        dv_c = (g_c * e_c).astype(BF16)
        scaled[:, cols] = sc
        dv[:, cols] = dv_c
        local[0, c] = dot(bt[...], sc)
        local[1, c] = dot(ct[...], dv_c)
        rows[0:1, cols] = e_c[span - 1 :, :]
        rows[2:3, cols] = dot(skip_pack[0:16], spread_c)[0:1]
        rows[4:5, cols] = jnp.sum(x_c * g_c, 0, keepdims=True)

        @pl.when(place == 0)
        def _():
            step(0, c, True)

        @pl.when(place == pairs - 1)
        def _():
            step(1, c, True)

        return carry

    lax.fori_loop(0, chunks, prepare, 0)

    def inner(j, carry):
        cols = pl.ds(pl.multiple_of(j * 2 * size, 2 * size), 2 * size)
        x2 = x_ref[:, cols]
        g2 = g_ref[:, cols]
        lane = lax.broadcasted_iota(jnp.int32, (span, 2 * size), 1)
        lower = t_row >= t_col
        y2, dx2 = [], []
        total = dcb[...]
        for i in range(2):
            h = 2 * j + i
            pick_row = lax.broadcasted_iota(jnp.int32, (LANES, span), 0)
            pick = jnp.where(lax.rem(pick_row, heads) == h, 1.0, 0.0).astype(BF16)
            at_t = dot(cum_pack[...], pick)
            decay = jnp.exp(jnp.where(lower, at_t - cum_rows[pl.ds(h, 1), :], -1e30))
            weights = (cb_ref[...] * decay).astype(BF16)
            y2.append(dot(weights, x2))
            dx2.append(dot(weights, g2, 0, 0))
            own_lanes = (lane < size) if i == 0 else (lane >= size)
            g_own = jnp.where(own_lanes, g2.astype(F32), 0.0).astype(BF16)
            total = total + dot(g_own, x2, 1, 1) * decay
        dcb[...] = total
        y_acc[:, cols] = jnp.where(lane < size, y2[0], y2[1])
        dx_acc[:, cols] = jnp.where(lane < size, dx2[0], dx2[1])
        return carry

    per_chunk = width // (2 * size)
    upper_half = jnp.where(place >= pairs // 2, 1, 0)

    def middle(c, carry):
        for s in range(2):
            d = upper_half + s - 2 * s * upper_half
            _, steps, _ = role(d)

            @pl.when(steps > 0)
            def _():
                step(d, c, False)

        return lax.fori_loop(c * per_chunk, (c + 1) * per_chunk, inner, carry)

    lax.fori_loop(0, chunks, middle, 0)

    dcb_low = dcb[...]
    dc_acc[...] = dot(dcb_low.astype(BF16), b_ref[...])
    db_acc[...] = dot(jnp.transpose(dcb_low).astype(BF16), c_ref[...])
    dcum[...] = jnp.zeros_like(dcum)

    def entering(d, c):
        lead, steps, lead_row = role(d)
        nothing = jnp.logical_and(lead, steps == 0)

        @pl.when(nothing)
        def _():
            m_in[d, c] = jnp.zeros((LANES, width), F32)

        @pl.when(jnp.logical_not(nothing))
        def _():
            m_copy(d, c).wait_recv()

        factor = jnp.where(lead_row, 1.0, rows[1:2, part(c)])
        return factor * p_in[d, c] + m_in[d, c]

    def finish(c, carry):
        cols = part(c)
        state = entering(0, c)
        adj = entering(1, c)
        state_low = state.astype(BF16)
        adj_low = adj.astype(BF16)
        x_c = x_ref[:, cols].astype(F32)
        g_c = g_ref[:, cols].astype(F32)
        skip_c = rows[2:3, cols]
        y_c = y_acc[:, cols] + e_wide[:, cols] * dot(c_ref[...], state_low)
        y_ref[:, cols] = (y_c + skip_c * x_c).astype(BF16)
        dx_state = to_wide[:, cols] * dot(b_ref[...], adj_low)
        dx_c = dx_acc[:, cols] + dx_state
        gx_ref[:, cols] = (dx_c + skip_c * g_c).astype(BF16)
        dc_acc[...] += dot(dv[:, cols], state_low, 1, 1)
        db_acc[...] += dot(scaled[:, cols], adj_low, 1, 1)
        hi, low = halves(g_c * y_c - x_c * dx_c)
        sel = spread[0:heads, cols]
        dcum[...] += dot(sel, hi, 1, 1) + dot(sel, low, 1, 1)
        rows[3:4, cols] = jnp.sum(x_c * dx_state, 0, keepdims=True) + rows[0:1, cols] * jnp.sum(
            state * adj, 0, keepdims=True
        )
        return carry

    lax.fori_loop(0, chunks, finish, 0)

    gc_ref[...] = dc_acc[...].astype(BF16)
    gb_ref[...] = db_acc[...].astype(BF16)
    sums = jnp.concatenate([rows[3:5, :], jnp.zeros((14, feat), F32)], 0)
    hi, low = halves(sums)
    sel = spread[0:heads, :]
    per_head = dot(sel, hi, 1, 1) + dot(sel, low, 1, 1)
    lower_f = jnp.where(t_row >= t_col, 1.0, 0.0).astype(F32)
    dla = dot(dcum[...], lower_f, precision=lax.Precision.HIGHEST) + per_head[:, 0:1]
    gdt_ref[...] = -rate * dla
    alog_row = as_row(jnp.sum(dla * la, 1, keepdims=True))
    skip_row = as_row(per_head[:, 1:2])

    stores = [
        pltpu.make_async_copy(src, dst, store_sem.at[i])
        for i, (src, dst) in enumerate(
            [
                (y_ref, y_hbm),
                (gx_ref, gx_hbm),
                (gb_ref, gb_hbm),
                (gc_ref, gc_hbm),
                (gdt_ref, gdt_hbm),
            ]
        )
    ]
    for move in stores:
        move.start()
    red_seq[me] = jnp.zeros((8, LANES), F32)
    red_seq[me, 0:1, 0:heads] = alog_row
    red_seq[me, 1:2, 0:heads] = skip_row

    def share(axis, here, count, buf, send, recv):
        def copy(target, slot, o):
            return pltpu.make_async_remote_copy(
                src_ref=buf.at[here],
                dst_ref=buf.at[slot],
                send_sem=send.at[o],
                recv_sem=recv.at[slot],
                device_id={axis: target},
                device_id_type=MESH,
            )

        def go(o, carry):
            copy(lax.rem(here + o, count), here, o).start()
            return carry

        def come(o, carry):
            source = lax.rem(here + o, count)
            copy(source, source, o).wait_recv()
            copy(source, here, o).wait_send()
            return carry

        lax.fori_loop(1, count, go, 0)
        lax.fori_loop(1, count, come, 0)
        return jnp.sum(buf[...], 0)

    red_dp[mine] = share("seq", me, n_seq, red_seq, rs_send, rs_recv)
    total = share("dp", mine, n_dp, red_dp, rd_send, rd_recv)
    ga_ref[...] = total[0:1, 0:heads]
    gs_ref[...] = total[1:2, 0:heads]

    def drain(c, carry):
        for d in range(2):
            lead, steps, _ = role(d)

            @pl.when(steps < pairs - 1)
            def _():
                p_copy(d, c).wait_send()

            @pl.when(jnp.logical_or(lead, steps > 0))
            def _():
                m_copy(d, c).wait_send()

        return carry

    lax.fori_loop(0, chunks, drain, 0)
    for move in stores:
        move.wait()


def write_out(count, *refs):
    sems = refs[-1]
    copies = [
        pltpu.make_async_copy(refs[i], refs[count + i], sems.at[i]) for i in range(count)
    ]
    for copy in copies:
        copy.start()
    for copy in copies:
        copy.wait()


def shards(n_seq, n_dp, x_in, b_in, c_in, dt, a_log, skip, cotangent):
    _, span, feat = x_in.shape
    state_dim = b_in.shape[2]
    heads = a_log.shape[0]
    width = 256
    chunks = feat // width
    blocks = (2, chunks, state_dim, width)
    vmem = pl.BlockSpec(memory_space=pltpu.VMEM)
    hbm = pl.BlockSpec(memory_space=pltpu.HBM)
    dma = pltpu.SemaphoreType.DMA
    wide = pltpu.VMEM((span, feat), F32)
    wide_low = pltpu.VMEM((span, feat), BF16)
    outs = pl.pallas_call(
        functools.partial(kernel, n_seq, n_dp, width),
        out_shape=(
            jax.ShapeDtypeStruct((span, feat), BF16),
            jax.ShapeDtypeStruct((span, feat), BF16),
            jax.ShapeDtypeStruct((span, state_dim), BF16),
            jax.ShapeDtypeStruct((span, state_dim), BF16),
            jax.ShapeDtypeStruct((heads, span), F32),
            jax.ShapeDtypeStruct((1, heads), F32),
            jax.ShapeDtypeStruct((1, heads), F32),
        ),
        in_specs=[hbm] * 7,
        out_specs=(hbm,) * 5 + (vmem,) * 2,
        scratch_shapes=[
            wide_low,
            wide_low,
            pltpu.VMEM((span, state_dim), BF16),
            pltpu.VMEM((span, state_dim), BF16),
            pltpu.VMEM((heads, span), F32),
            wide_low,
            pltpu.VMEM((span, state_dim), BF16),
            pltpu.VMEM((span, state_dim), BF16),
            pltpu.VMEM((heads, span), F32),
            pltpu.VMEM((1, heads), F32),
            pltpu.VMEM((1, heads), F32),
            wide_low,
            pltpu.VMEM((LANES, feat), BF16),
            pltpu.VMEM((LANES, span), F32),
            pltpu.VMEM((span, LANES), BF16),
            wide,
            wide,
            wide_low,
            wide_low,
            pltpu.VMEM((state_dim, span), BF16),
            pltpu.VMEM((state_dim, span), BF16),
            pltpu.VMEM(blocks, F32),
            pltpu.VMEM(blocks, F32),
            pltpu.VMEM(blocks, F32),
            pltpu.VMEM(blocks, F32),
            pltpu.VMEM(blocks, F32),
            pltpu.VMEM((8, feat), F32),
            wide,
            wide,
            pltpu.VMEM((span, span), F32),
            pltpu.VMEM((span, span), F32),
            pltpu.VMEM((span, state_dim), F32),
            pltpu.VMEM((span, state_dim), F32),
            pltpu.VMEM((heads, span), F32),
            pltpu.VMEM((16, LANES), F32),
            pltpu.VMEM((16, LANES), F32),
            pltpu.VMEM((n_seq, 8, LANES), F32),
            pltpu.VMEM((n_dp, 8, LANES), F32),
            dma((2, chunks)),
            dma((2, chunks)),
            dma((2, chunks)),
            dma((2, chunks)),
            dma((2,)),
            dma((7,)),
            dma((5,)),
            dma((n_seq,)),
            dma((n_seq,)),
            dma((n_dp,)),
            dma((n_dp,)),
        ],
        compiler_params=pltpu.CompilerParams(
            collective_id=0, has_side_effects=True, vmem_limit_bytes=VMEM_BYTES
        ),
    )(x_in[0], b_in[0], c_in[0], dt[0], a_log[None], skip[None], cotangent[0])
    y, gx, gb, gc, gdt, ga, gs = pl.pallas_call(
        functools.partial(write_out, len(outs)),
        out_shape=tuple(jax.ShapeDtypeStruct(o.shape, o.dtype) for o in outs),
        in_specs=[hbm] * len(outs),
        out_specs=(hbm,) * len(outs),
        scratch_shapes=[dma((len(outs),))],
        compiler_params=pltpu.CompilerParams(vmem_limit_bytes=VMEM_BYTES),
    )(*outs)
    return (y[None], gx[None], gb[None], gc[None], gdt[None], ga[0], gs[0])


def solution(mesh):
    tokens = P("dp", "seq", None)
    steps = P("dp", None, "seq")
    return jax.shard_map(
        functools.partial(shards, mesh.shape["seq"], mesh.shape["dp"]),
        mesh=mesh,
        in_specs=(tokens, tokens, tokens, steps, P(), P(), tokens),
        out_specs=(tokens, tokens, tokens, tokens, steps, P(), P()),
        check_vma=False,
    )
```

```python
import functools

import jax
import jax.numpy as jnp
from jax import lax
from jax.experimental import pallas as pl
from jax.experimental.pallas import tpu as pltpu
from jax.sharding import PartitionSpec as P

F32 = jnp.float32
BF16 = jnp.bfloat16
MESH = pl.DeviceIdType.MESH
LANES = 128
VMEM_BYTES = 62 * 1024 * 1024


def dot(a, b, ca=1, cb=0, precision=None):
    return lax.dot_general(
        a, b, (((ca,), (cb,)), ((), ())), preferred_element_type=F32, precision=precision
    )


def pack(v, heads):
    lane = lax.broadcasted_iota(jnp.int32, v.shape, 1)
    hi = v.astype(BF16).astype(F32)
    rest = v - hi
    mid = rest.astype(BF16).astype(F32)
    low = rest - mid
    out = jnp.where(lane < heads, hi, jnp.where(lane < 2 * heads, mid, low))
    return jnp.where(lane < 3 * heads, out, 0.0).astype(BF16)


def halves(v):
    hi = v.astype(BF16)
    return hi, (v - hi.astype(F32)).astype(BF16)


def kernel(
    n_seq,
    n_dp,
    width,
    x_hbm,
    b_hbm,
    c_hbm,
    dt_hbm,
    alog_hbm,
    skip_hbm,
    g_hbm,
    y_hbm,
    gx_hbm,
    gb_hbm,
    gc_hbm,
    gdt_hbm,
    ga_ref,
    gs_ref,
    y_ref,
    gx_ref,
    gb_ref,
    gc_ref,
    gdt_ref,
    x_ref,
    b_ref,
    c_ref,
    dt_ref,
    alog_ref,
    skip_ref,
    g_ref,
    spread,
    cum_rows,
    cum_pack,
    e_wide,
    to_wide,
    scaled,
    dv,
    bt,
    ct,
    local,
    p_in,
    p_out,
    m_in,
    m_out,
    rows,
    y_acc,
    dx_acc,
    cb_ref,
    dcb,
    dc_acc,
    db_acc,
    dcum,
    gain_own,
    gain_in,
    red_seq,
    red_dp,
    p_send,
    p_recv,
    m_send,
    m_recv,
    g_sem,
    load_sem,
    store_sem,
    rs_send,
    rs_recv,
    rd_send,
    rd_recv,
):
    heads, span = dt_ref.shape
    feat = x_ref.shape[1]
    size = feat // heads
    chunks = feat // width
    pairs = n_seq // 2
    me = lax.axis_index("seq")
    mine = lax.axis_index("dp")
    place = me // 2
    odd = lax.rem(me, 2)
    partner = me + 1 - 2 * odd

    moves = [
        pltpu.make_async_copy(src, dst, load_sem.at[i])
        for i, (src, dst) in enumerate(
            [
                (dt_hbm, dt_ref),
                (alog_hbm, alog_ref),
                (skip_hbm, skip_ref),
                (b_hbm, b_ref),
                (c_hbm, c_ref),
                (x_hbm, x_ref),
                (g_hbm, g_ref),
            ]
        )
    ]
    for move in moves:
        move.start()
    barrier = pltpu.get_barrier_semaphore()

    def greet_seq(o, carry):
        pl.semaphore_signal(
            barrier, inc=1, device_id={"seq": lax.rem(me + o, n_seq)}, device_id_type=MESH
        )
        return carry

    def greet_dp(o, carry):
        pl.semaphore_signal(
            barrier, inc=1, device_id={"dp": lax.rem(mine + o, n_dp)}, device_id_type=MESH
        )
        return carry

    lax.fori_loop(1, n_seq, greet_seq, 0)
    lax.fori_loop(1, n_dp, greet_dp, 0)

    diag = lax.broadcasted_iota(jnp.int32, (heads, heads), 0) == lax.broadcasted_iota(
        jnp.int32, (heads, heads), 1
    )

    def column(row):
        return jnp.sum(jnp.where(diag, jnp.broadcast_to(row, (heads, heads)), 0.0), 1, keepdims=True)

    def as_row(col):
        return jnp.sum(jnp.where(diag, jnp.broadcast_to(col, (heads, heads)), 0.0), 0, keepdims=True)

    for move in moves[:3]:
        move.wait()
    rate = jnp.exp(column(alog_ref[...]))
    la = -rate * dt_ref[...]
    t_row = lax.broadcasted_iota(jnp.int32, (span, span), 0)
    t_col = lax.broadcasted_iota(jnp.int32, (span, span), 1)
    upper = jnp.where(t_row <= t_col, 1.0, 0.0).astype(F32)
    cum = dot(jnp.concatenate([la] * (LANES // heads), 0), upper, precision=lax.Precision.HIGHEST)
    cum_rows[...] = cum
    cum_t = jnp.transpose(cum)
    cum_pack[...] = pack(cum_t, heads)
    e_t = jnp.exp(cum_t)
    gain_own[...] = e_t[span - 16 :, :]
    pl.semaphore_wait(barrier, n_seq - 1 + n_dp - 1)
    gain_copy = pltpu.make_async_remote_copy(
        src_ref=gain_own,
        dst_ref=gain_in,
        send_sem=g_sem.at[0],
        recv_sem=g_sem.at[1],
        device_id={"seq": partner},
        device_id_type=MESH,
    )
    gain_copy.start()

    e_pack = pack(e_t, heads)
    to_pack = pack(jnp.exp(cum_t[span - 1 :, :] - cum_t), heads)
    spread_row = lax.rem(lax.broadcasted_iota(jnp.int32, spread.shape, 0), heads)
    spread_col = lax.broadcasted_iota(jnp.int32, spread.shape, 1) // size
    spread[...] = jnp.where(spread_row == spread_col, 1.0, 0.0).astype(BF16)
    for move in moves[3:]:
        move.wait()
    bt[...] = jnp.transpose(b_ref[...].astype(F32)).astype(BF16)
    ct[...] = jnp.transpose(c_ref[...].astype(F32)).astype(BF16)
    skip_col = jnp.broadcast_to(column(skip_ref[...]), (heads, LANES))
    skip_pack = pack(jnp.transpose(jnp.concatenate([skip_col] * (LANES // heads), 0)), heads)

    def part(c):
        return pl.ds(pl.multiple_of(c * width, width), width)

    cb_ref[...] = dot(c_ref[...], b_ref[...], 1, 1)
    dcb[...] = jnp.zeros_like(dcb)

    gain_copy.wait()
    gain_pack = pack(gain_in[...], heads)
    rows[1:2, :] = dot(gain_pack, spread[...])[15:16, :]

    def role(d):
        lead = odd == d
        steps = jnp.where(d == 0, place, pairs - 1 - place)
        lead_row = jnp.broadcast_to(jnp.where(lead, 1, 0), (1, width)) == 1
        return lead, steps, lead_row

    def p_copy(d, c):
        return pltpu.make_async_remote_copy(
            src_ref=p_out.at[d, c],
            dst_ref=p_in.at[d, c],
            send_sem=p_send.at[d, c],
            recv_sem=p_recv.at[d, c],
            device_id={"seq": lax.rem(me + 2 - 4 * d + n_seq, n_seq)},
            device_id_type=MESH,
        )

    def m_copy(d, c):
        return pltpu.make_async_remote_copy(
            src_ref=m_out.at[d, c],
            dst_ref=m_in.at[d, c],
            send_sem=m_send.at[d, c],
            recv_sem=m_recv.at[d, c],
            device_id={"seq": partner},
            device_id_type=MESH,
        )

    def step(d, c, at_start):
        lead, steps, lead_row = role(d)
        cols = part(c)
        own = rows[0:1, cols]
        other = rows[1:2, cols]
        here = local[d, c]
        if at_start:
            p_in[d, c] = jnp.zeros_like(here)

            @pl.when(lead)
            def _():
                m_out[d, c] = here
                m_copy(d, c).start()

            p_out[d, c] = jnp.where(lead_row, other, 1.0) * here
            p_copy(d, c).start()
        else:
            p_copy(d, c).wait_recv()
            before = p_in[d, c]

            @pl.when(steps < pairs - 1)
            def _():
                p_out[d, c] = own * other * before + jnp.where(lead_row, other, 1.0) * here
                p_copy(d, c).start()

            m_out[d, c] = jnp.where(lead_row, own, 1.0) * before + jnp.where(lead_row, here, 0.0)
            m_copy(d, c).start()

    def prepare(c, carry):
        cols = part(c)
        spread_c = spread[:, cols]
        e_c = dot(e_pack, spread_c)
        to_c = dot(to_pack, spread_c)
        e_wide[:, cols] = e_c
        to_wide[:, cols] = to_c
        x_c = x_ref[:, cols].astype(F32)
        g_c = g_ref[:, cols].astype(F32)
        sc = (x_c * to_c).astype(BF16)
        dv_c = (g_c * e_c).astype(BF16)
        scaled[:, cols] = sc
        dv[:, cols] = dv_c
        local[0, c] = dot(bt[...], sc)
        local[1, c] = dot(ct[...], dv_c)
        rows[0:1, cols] = e_c[span - 1 :, :]
        rows[2:3, cols] = dot(skip_pack[0:16], spread_c)[0:1]
        rows[4:5, cols] = jnp.sum(x_c * g_c, 0, keepdims=True)

        @pl.when(place == 0)
        def _():
            step(0, c, True)

        @pl.when(place == pairs - 1)
        def _():
            step(1, c, True)

        return carry

    lax.fori_loop(0, chunks, prepare, 0)

    def inner(j, carry):
        cols = pl.ds(pl.multiple_of(j * 2 * size, 2 * size), 2 * size)
        x2 = x_ref[:, cols]
        g2 = g_ref[:, cols]
        lane = lax.broadcasted_iota(jnp.int32, (span, 2 * size), 1)
        lower = t_row >= t_col
        y2, dx2 = [], []
        total = dcb[...]
        for i in range(2):
            h = 2 * j + i
            pick_row = lax.broadcasted_iota(jnp.int32, (LANES, span), 0)
            pick = jnp.where(lax.rem(pick_row, heads) == h, 1.0, 0.0).astype(BF16)
            at_t = dot(cum_pack[...], pick)
            decay = jnp.exp(jnp.where(lower, at_t - cum_rows[pl.ds(h, 1), :], -1e30))
            weights = (cb_ref[...] * decay).astype(BF16)
            y2.append(dot(weights, x2))
            dx2.append(dot(weights, g2, 0, 0))
            own_lanes = (lane < size) if i == 0 else (lane >= size)
            g_own = jnp.where(own_lanes, g2.astype(F32), 0.0).astype(BF16)
            total = total + dot(g_own, x2, 1, 1) * decay
        dcb[...] = total
        y_acc[:, cols] = jnp.where(lane < size, y2[0], y2[1])
        dx_acc[:, cols] = jnp.where(lane < size, dx2[0], dx2[1])
        return carry

    per_chunk = width // (2 * size)
    upper_half = jnp.where(place >= pairs // 2, 1, 0)

    def onward(d, c):
        _, steps, _ = role(d)

        @pl.when(steps > 0)
        def _():
            step(d, c, False)

    def middle(c, carry):
        onward(upper_half, c)
        lax.fori_loop(c * per_chunk, (c + 1) * per_chunk, inner, 0)
        onward(1 - upper_half, c)
        return carry

    lax.fori_loop(0, chunks, middle, 0)

    dcb_low = dcb[...]
    dc_acc[...] = dot(dcb_low.astype(BF16), b_ref[...])
    db_acc[...] = dot(jnp.transpose(dcb_low).astype(BF16), c_ref[...])
    dcum[...] = jnp.zeros_like(dcum)

    def entering(d, c):
        lead, steps, lead_row = role(d)
        nothing = jnp.logical_and(lead, steps == 0)

        @pl.when(nothing)
        def _():
            m_in[d, c] = jnp.zeros((LANES, width), F32)

        @pl.when(jnp.logical_not(nothing))
        def _():
            m_copy(d, c).wait_recv()

        factor = jnp.where(lead_row, 1.0, rows[1:2, part(c)])
        return factor * p_in[d, c] + m_in[d, c]

    def finish(c, carry):
        cols = part(c)
        state = entering(0, c)
        adj = entering(1, c)
        state_low = state.astype(BF16)
        adj_low = adj.astype(BF16)
        x_c = x_ref[:, cols].astype(F32)
        g_c = g_ref[:, cols].astype(F32)
        skip_c = rows[2:3, cols]
        y_c = y_acc[:, cols] + e_wide[:, cols] * dot(c_ref[...], state_low)
        y_ref[:, cols] = (y_c + skip_c * x_c).astype(BF16)
        dx_state = to_wide[:, cols] * dot(b_ref[...], adj_low)
        dx_c = dx_acc[:, cols] + dx_state
        gx_ref[:, cols] = (dx_c + skip_c * g_c).astype(BF16)
        dc_acc[...] += dot(dv[:, cols], state_low, 1, 1)
        db_acc[...] += dot(scaled[:, cols], adj_low, 1, 1)
        hi, low = halves(g_c * y_c - x_c * dx_c)
        sel = spread[0:heads, cols]
        dcum[...] += dot(sel, hi, 1, 1) + dot(sel, low, 1, 1)
        rows[3:4, cols] = jnp.sum(x_c * dx_state, 0, keepdims=True) + rows[0:1, cols] * jnp.sum(
            state * adj, 0, keepdims=True
        )
        return carry

    lax.fori_loop(0, chunks, finish, 0)

    gc_ref[...] = dc_acc[...].astype(BF16)
    gb_ref[...] = db_acc[...].astype(BF16)
    sums = jnp.concatenate([rows[3:5, :], jnp.zeros((14, feat), F32)], 0)
    hi, low = halves(sums)
    sel = spread[0:heads, :]
    per_head = dot(sel, hi, 1, 1) + dot(sel, low, 1, 1)
    lower_f = jnp.where(t_row >= t_col, 1.0, 0.0).astype(F32)
    dla = dot(dcum[...], lower_f, precision=lax.Precision.HIGHEST) + per_head[:, 0:1]
    gdt_ref[...] = -rate * dla
    alog_row = as_row(jnp.sum(dla * la, 1, keepdims=True))
    skip_row = as_row(per_head[:, 1:2])

    stores = [
        pltpu.make_async_copy(src, dst, store_sem.at[i])
        for i, (src, dst) in enumerate(
            [
                (y_ref, y_hbm),
                (gx_ref, gx_hbm),
                (gb_ref, gb_hbm),
                (gc_ref, gc_hbm),
                (gdt_ref, gdt_hbm),
            ]
        )
    ]
    for move in stores:
        move.start()
    red_seq[me] = jnp.zeros((8, LANES), F32)
    red_seq[me, 0:1, 0:heads] = alog_row
    red_seq[me, 1:2, 0:heads] = skip_row

    def share(axis, here, count, buf, send, recv):
        def copy(target, slot, o):
            return pltpu.make_async_remote_copy(
                src_ref=buf.at[here],
                dst_ref=buf.at[slot],
                send_sem=send.at[o],
                recv_sem=recv.at[slot],
                device_id={axis: target},
                device_id_type=MESH,
            )

        def go(o, carry):
            copy(lax.rem(here + o, count), here, o).start()
            return carry

        def come(o, carry):
            source = lax.rem(here + o, count)
            copy(source, source, o).wait_recv()
            copy(source, here, o).wait_send()
            return carry

        lax.fori_loop(1, count, go, 0)
        lax.fori_loop(1, count, come, 0)
        return jnp.sum(buf[...], 0)

    red_dp[mine] = share("seq", me, n_seq, red_seq, rs_send, rs_recv)
    total = share("dp", mine, n_dp, red_dp, rd_send, rd_recv)
    ga_ref[...] = total[0:1, 0:heads]
    gs_ref[...] = total[1:2, 0:heads]

    def drain(c, carry):
        for d in range(2):
            lead, steps, _ = role(d)

            @pl.when(steps < pairs - 1)
            def _():
                p_copy(d, c).wait_send()

            @pl.when(jnp.logical_or(lead, steps > 0))
            def _():
                m_copy(d, c).wait_send()

        return carry

    lax.fori_loop(0, chunks, drain, 0)
    for move in stores:
        move.wait()


def write_out(count, *refs):
    held = refs[2 * count : 3 * count]
    load, store = refs[3 * count :]
    loads = [pltpu.make_async_copy(refs[i], held[i], load.at[i]) for i in range(count)]
    stores = [
        pltpu.make_async_copy(held[i], refs[count + i], store.at[i]) for i in range(count)
    ]
    for copy in loads:
        copy.start()
    for first, second in zip(loads, stores):
        first.wait()
        second.start()
    for copy in stores:
        copy.wait()


def shards(n_seq, n_dp, x_in, b_in, c_in, dt, a_log, skip, cotangent):
    _, span, feat = x_in.shape
    state_dim = b_in.shape[2]
    heads = a_log.shape[0]
    width = 256
    chunks = feat // width
    blocks = (2, chunks, state_dim, width)
    vmem = pl.BlockSpec(memory_space=pltpu.VMEM)
    hbm = pl.BlockSpec(memory_space=pltpu.HBM)
    dma = pltpu.SemaphoreType.DMA
    wide = pltpu.VMEM((span, feat), F32)
    wide_low = pltpu.VMEM((span, feat), BF16)
    outs = pl.pallas_call(
        functools.partial(kernel, n_seq, n_dp, width),
        out_shape=(
            jax.ShapeDtypeStruct((span, feat), BF16),
            jax.ShapeDtypeStruct((span, feat), BF16),
            jax.ShapeDtypeStruct((span, state_dim), BF16),
            jax.ShapeDtypeStruct((span, state_dim), BF16),
            jax.ShapeDtypeStruct((heads, span), F32),
            jax.ShapeDtypeStruct((1, heads), F32),
            jax.ShapeDtypeStruct((1, heads), F32),
        ),
        in_specs=[hbm] * 7,
        out_specs=(hbm,) * 5 + (vmem,) * 2,
        scratch_shapes=[
            wide_low,
            wide_low,
            pltpu.VMEM((span, state_dim), BF16),
            pltpu.VMEM((span, state_dim), BF16),
            pltpu.VMEM((heads, span), F32),
            wide_low,
            pltpu.VMEM((span, state_dim), BF16),
            pltpu.VMEM((span, state_dim), BF16),
            pltpu.VMEM((heads, span), F32),
            pltpu.VMEM((1, heads), F32),
            pltpu.VMEM((1, heads), F32),
            wide_low,
            pltpu.VMEM((LANES, feat), BF16),
            pltpu.VMEM((LANES, span), F32),
            pltpu.VMEM((span, LANES), BF16),
            wide,
            wide,
            wide_low,
            wide_low,
            pltpu.VMEM((state_dim, span), BF16),
            pltpu.VMEM((state_dim, span), BF16),
            pltpu.VMEM(blocks, F32),
            pltpu.VMEM(blocks, F32),
            pltpu.VMEM(blocks, F32),
            pltpu.VMEM(blocks, F32),
            pltpu.VMEM(blocks, F32),
            pltpu.VMEM((8, feat), F32),
            wide,
            wide,
            pltpu.VMEM((span, span), F32),
            pltpu.VMEM((span, span), F32),
            pltpu.VMEM((span, state_dim), F32),
            pltpu.VMEM((span, state_dim), F32),
            pltpu.VMEM((heads, span), F32),
            pltpu.VMEM((16, LANES), F32),
            pltpu.VMEM((16, LANES), F32),
            pltpu.VMEM((n_seq, 8, LANES), F32),
            pltpu.VMEM((n_dp, 8, LANES), F32),
            dma((2, chunks)),
            dma((2, chunks)),
            dma((2, chunks)),
            dma((2, chunks)),
            dma((2,)),
            dma((7,)),
            dma((5,)),
            dma((n_seq,)),
            dma((n_seq,)),
            dma((n_dp,)),
            dma((n_dp,)),
        ],
        compiler_params=pltpu.CompilerParams(
            collective_id=0, has_side_effects=True, vmem_limit_bytes=VMEM_BYTES
        ),
    )(x_in[0], b_in[0], c_in[0], dt[0], a_log[None], skip[None], cotangent[0])
    y, gx, gb, gc, gdt, ga, gs = pl.pallas_call(
        functools.partial(write_out, len(outs)),
        out_shape=tuple(jax.ShapeDtypeStruct(o.shape, o.dtype) for o in outs),
        in_specs=[hbm] * len(outs),
        out_specs=(hbm,) * len(outs),
        scratch_shapes=[pltpu.VMEM(o.shape, o.dtype) for o in outs]
        + [dma((len(outs),)), dma((len(outs),))],
        compiler_params=pltpu.CompilerParams(vmem_limit_bytes=VMEM_BYTES),
    )(*outs)
    return (y[None], gx[None], gb[None], gc[None], gdt[None], ga[0], gs[0])


def solution(mesh):
    tokens = P("dp", "seq", None)
    steps = P("dp", None, "seq")
    return jax.shard_map(
        functools.partial(shards, mesh.shape["seq"], mesh.shape["dp"]),
        mesh=mesh,
        in_specs=(tokens, tokens, tokens, steps, P(), P(), tokens),
        out_specs=(tokens, tokens, tokens, tokens, steps, P(), P()),
        check_vma=False,
    )
```

```python
import functools

import jax
import jax.numpy as jnp
from jax import lax
from jax.experimental import pallas as pl
from jax.experimental.pallas import tpu as pltpu
from jax.sharding import PartitionSpec as P

F32 = jnp.float32
BF16 = jnp.bfloat16
MESH = pl.DeviceIdType.MESH
LANES = 128
VMEM_BYTES = 62 * 1024 * 1024


def dot(a, b, ca=1, cb=0, precision=None):
    return lax.dot_general(
        a, b, (((ca,), (cb,)), ((), ())), preferred_element_type=F32, precision=precision
    )


def pack(v, heads):
    lane = lax.broadcasted_iota(jnp.int32, v.shape, 1)
    hi = v.astype(BF16).astype(F32)
    rest = v - hi
    mid = rest.astype(BF16).astype(F32)
    low = rest - mid
    out = jnp.where(lane < heads, hi, jnp.where(lane < 2 * heads, mid, low))
    return jnp.where(lane < 3 * heads, out, 0.0).astype(BF16)


def halves(v):
    hi = v.astype(BF16)
    return hi, (v - hi.astype(F32)).astype(BF16)


def kernel(
    n_seq,
    n_dp,
    width,
    x_hbm,
    b_hbm,
    c_hbm,
    dt_hbm,
    alog_hbm,
    skip_hbm,
    g_hbm,
    y_hbm,
    gx_hbm,
    gb_hbm,
    gc_hbm,
    gdt_hbm,
    ga_ref,
    gs_ref,
    y_ref,
    gx_ref,
    gb_ref,
    gc_ref,
    gdt_ref,
    x_ref,
    b_ref,
    c_ref,
    dt_ref,
    alog_ref,
    skip_ref,
    g_ref,
    spread,
    cum_rows,
    cum_pack,
    e_wide,
    to_wide,
    scaled,
    dv,
    bt,
    ct,
    local,
    p_in,
    p_out,
    other_local,
    entry,
    m_out,
    rows,
    y_acc,
    dx_acc,
    cb_ref,
    dcb,
    dc_acc,
    db_acc,
    dcum,
    gain_own,
    gain_in,
    red_seq,
    red_dp,
    p_send,
    p_recv,
    m_send,
    m_recv,
    l_send,
    l_recv,
    g_sem,
    load_sem,
    store_sem,
    rs_send,
    rs_recv,
    rd_send,
    rd_recv,
):
    heads, span = dt_ref.shape
    feat = x_ref.shape[1]
    size = feat // heads
    chunks = feat // width
    pairs = n_seq // 2
    me = lax.axis_index("seq")
    mine = lax.axis_index("dp")
    place = me // 2
    odd = lax.rem(me, 2)
    partner = me + 1 - 2 * odd

    moves = [
        pltpu.make_async_copy(src, dst, load_sem.at[i])
        for i, (src, dst) in enumerate(
            [
                (dt_hbm, dt_ref),
                (alog_hbm, alog_ref),
                (skip_hbm, skip_ref),
                (b_hbm, b_ref),
                (c_hbm, c_ref),
                (x_hbm, x_ref),
                (g_hbm, g_ref),
            ]
        )
    ]
    for move in moves:
        move.start()
    barrier = pltpu.get_barrier_semaphore()

    def greet_seq(o, carry):
        pl.semaphore_signal(
            barrier, inc=1, device_id={"seq": lax.rem(me + o, n_seq)}, device_id_type=MESH
        )
        return carry

    def greet_dp(o, carry):
        pl.semaphore_signal(
            barrier, inc=1, device_id={"dp": lax.rem(mine + o, n_dp)}, device_id_type=MESH
        )
        return carry

    lax.fori_loop(1, n_seq, greet_seq, 0)
    lax.fori_loop(1, n_dp, greet_dp, 0)

    diag = lax.broadcasted_iota(jnp.int32, (heads, heads), 0) == lax.broadcasted_iota(
        jnp.int32, (heads, heads), 1
    )

    def column(row):
        return jnp.sum(jnp.where(diag, jnp.broadcast_to(row, (heads, heads)), 0.0), 1, keepdims=True)

    def as_row(col):
        return jnp.sum(jnp.where(diag, jnp.broadcast_to(col, (heads, heads)), 0.0), 0, keepdims=True)

    for move in moves[:3]:
        move.wait()
    rate = jnp.exp(column(alog_ref[...]))
    la = -rate * dt_ref[...]
    t_row = lax.broadcasted_iota(jnp.int32, (span, span), 0)
    t_col = lax.broadcasted_iota(jnp.int32, (span, span), 1)
    upper = jnp.where(t_row <= t_col, 1.0, 0.0).astype(F32)
    cum = dot(jnp.concatenate([la] * (LANES // heads), 0), upper, precision=lax.Precision.HIGHEST)
    cum_rows[...] = cum
    cum_t = jnp.transpose(cum)
    cum_pack[...] = pack(cum_t, heads)
    e_t = jnp.exp(cum_t)
    gain_own[...] = e_t[span - 16 :, :]
    pl.semaphore_wait(barrier, n_seq - 1 + n_dp - 1)
    gain_copy = pltpu.make_async_remote_copy(
        src_ref=gain_own,
        dst_ref=gain_in,
        send_sem=g_sem.at[0],
        recv_sem=g_sem.at[1],
        device_id={"seq": partner},
        device_id_type=MESH,
    )
    gain_copy.start()

    e_pack = pack(e_t, heads)
    to_pack = pack(jnp.exp(cum_t[span - 1 :, :] - cum_t), heads)
    spread_row = lax.rem(lax.broadcasted_iota(jnp.int32, spread.shape, 0), heads)
    spread_col = lax.broadcasted_iota(jnp.int32, spread.shape, 1) // size
    spread[...] = jnp.where(spread_row == spread_col, 1.0, 0.0).astype(BF16)
    for move in moves[3:]:
        move.wait()
    bt[...] = jnp.transpose(b_ref[...].astype(F32)).astype(BF16)
    ct[...] = jnp.transpose(c_ref[...].astype(F32)).astype(BF16)
    skip_col = jnp.broadcast_to(column(skip_ref[...]), (heads, LANES))
    skip_pack = pack(jnp.transpose(jnp.concatenate([skip_col] * (LANES // heads), 0)), heads)

    def part(c):
        return pl.ds(pl.multiple_of(c * width, width), width)

    cb_ref[...] = dot(c_ref[...], b_ref[...], 1, 1)
    dcb[...] = jnp.zeros_like(dcb)

    def role(d):
        lead = odd == d
        steps = jnp.where(d == 0, place, pairs - 1 - place)
        lead_row = jnp.broadcast_to(jnp.where(lead, 1, 0), (1, width)) == 1
        return lead, steps, lead_row

    def p_copy(d, c):
        return pltpu.make_async_remote_copy(
            src_ref=p_out.at[d, c],
            dst_ref=p_in.at[d, c],
            send_sem=p_send.at[d, c],
            recv_sem=p_recv.at[d, c],
            device_id={"seq": lax.rem(me + 2 - 4 * d + n_seq, n_seq)},
            device_id_type=MESH,
        )

    def m_copy(d, c):
        return pltpu.make_async_remote_copy(
            src_ref=m_out.at[d, c],
            dst_ref=entry.at[d, c],
            send_sem=m_send.at[d, c],
            recv_sem=m_recv.at[d, c],
            device_id={"seq": partner},
            device_id_type=MESH,
        )

    def l_copy(d, c):
        return pltpu.make_async_remote_copy(
            src_ref=local.at[d, c],
            dst_ref=other_local.at[d, c],
            send_sem=l_send.at[d, c],
            recv_sem=l_recv.at[d, c],
            device_id={"seq": partner},
            device_id_type=MESH,
        )

    half = chunks // 2
    blank = jnp.zeros((LANES, width), F32)

    def step(d, c):
        lead, steps, lead_row = role(d)
        cols = part(c)
        own = rows[0:1, cols]
        other = rows[1:2, cols]
        wanted = jnp.logical_or(jnp.logical_not(lead), steps < pairs - 1)

        @pl.when(wanted)
        def _():
            l_copy(d, c).wait_recv()

        @pl.when(jnp.logical_not(wanted))
        def _():
            other_local[d, c] = blank

        @pl.when(steps > 0)
        def _():
            p_copy(d, c).wait_recv()

        @pl.when(steps == 0)
        def _():
            p_in[d, c] = blank

        before = p_in[d, c]
        here = local[d, c]
        there = other_local[d, c]

        @pl.when(steps < pairs - 1)
        def _():
            p_out[d, c] = own * other * before + jnp.where(
                lead_row, other * here + there, own * there + here
            )
            p_copy(d, c).start()

        m_out[d, c] = jnp.where(lead_row, own * before + here, before)

        @pl.when(jnp.logical_or(lead, steps > 0))
        def _():
            m_copy(d, c).start()

        entry[d, c] = jnp.where(lead_row, before, other * before + there)

    def prepare(i, carry):
        c = lax.rem(i + (1 - odd) * half, chunks)
        cols = part(c)
        spread_c = spread[:, cols]
        e_c = dot(e_pack, spread_c)
        to_c = dot(to_pack, spread_c)
        e_wide[:, cols] = e_c
        to_wide[:, cols] = to_c
        x_c = x_ref[:, cols].astype(F32)
        g_c = g_ref[:, cols].astype(F32)
        sc = (x_c * to_c).astype(BF16)
        dv_c = (g_c * e_c).astype(BF16)
        scaled[:, cols] = sc
        dv[:, cols] = dv_c
        local[0, c] = dot(bt[...], sc)
        local[1, c] = dot(ct[...], dv_c)
        rows[0:1, cols] = e_c[span - 1 :, :]
        rows[2:3, cols] = dot(skip_pack[0:16], spread_c)[0:1]
        rows[4:5, cols] = jnp.sum(x_c * g_c, 0, keepdims=True)

        for d in range(2):
            lead, steps, _ = role(d)
            wanted = jnp.logical_or(lead, steps < pairs - 1)

            @pl.when(jnp.logical_and(i < half, wanted))
            def _():
                l_copy(d, c).start()

        return carry

    lax.fori_loop(0, chunks, prepare, 0)
    gain_copy.wait()
    gain_pack = pack(gain_in[...], heads)
    rows[1:2, :] = dot(gain_pack, spread[...])[15:16, :]


    def inner(j, carry):
        cols = pl.ds(pl.multiple_of(j * 2 * size, 2 * size), 2 * size)
        x2 = x_ref[:, cols]
        g2 = g_ref[:, cols]
        lane = lax.broadcasted_iota(jnp.int32, (span, 2 * size), 1)
        lower = t_row >= t_col
        y2, dx2 = [], []
        total = dcb[...]
        for i in range(2):
            h = 2 * j + i
            pick_row = lax.broadcasted_iota(jnp.int32, (LANES, span), 0)
            pick = jnp.where(lax.rem(pick_row, heads) == h, 1.0, 0.0).astype(BF16)
            at_t = dot(cum_pack[...], pick)
            decay = jnp.exp(jnp.where(lower, at_t - cum_rows[pl.ds(h, 1), :], -1e30))
            weights = (cb_ref[...] * decay).astype(BF16)
            y2.append(dot(weights, x2))
            dx2.append(dot(weights, g2, 0, 0))
            own_lanes = (lane < size) if i == 0 else (lane >= size)
            g_own = jnp.where(own_lanes, g2.astype(F32), 0.0).astype(BF16)
            total = total + dot(g_own, x2, 1, 1) * decay
        dcb[...] = total
        y_acc[:, cols] = jnp.where(lane < size, y2[0], y2[1])
        dx_acc[:, cols] = jnp.where(lane < size, dx2[0], dx2[1])
        return carry

    per_chunk = width // (2 * size)
    upper_half = jnp.where(place >= pairs // 2, 1, 0)

    def middle(i, carry):
        late = i // half
        step(upper_half + late - 2 * late * upper_half, lax.rem(i, half) + odd * half)
        return lax.fori_loop(i * per_chunk, (i + 1) * per_chunk, inner, carry)

    lax.fori_loop(0, chunks, middle, 0)

    dcb_low = dcb[...]
    dc_acc[...] = dot(dcb_low.astype(BF16), b_ref[...])
    db_acc[...] = dot(jnp.transpose(dcb_low).astype(BF16), c_ref[...])
    dcum[...] = jnp.zeros_like(dcum)

    def finish(i, carry):
        c = lax.rem(i + odd * half, chunks)
        cols = part(c)
        for d in range(2):
            lead, steps, _ = role(d)
            nothing = jnp.logical_and(lead, steps == 0)

            @pl.when(jnp.logical_and(i >= half, nothing))
            def _():
                entry[d, c] = blank

            @pl.when(jnp.logical_and(i >= half, jnp.logical_not(nothing)))
            def _():
                m_copy(d, c).wait_recv()

        state = entry[0, c]
        adj = entry[1, c]
        state_low = state.astype(BF16)
        adj_low = adj.astype(BF16)
        x_c = x_ref[:, cols].astype(F32)
        g_c = g_ref[:, cols].astype(F32)
        skip_c = rows[2:3, cols]
        y_c = y_acc[:, cols] + e_wide[:, cols] * dot(c_ref[...], state_low)
        y_ref[:, cols] = (y_c + skip_c * x_c).astype(BF16)
        dx_state = to_wide[:, cols] * dot(b_ref[...], adj_low)
        dx_c = dx_acc[:, cols] + dx_state
        gx_ref[:, cols] = (dx_c + skip_c * g_c).astype(BF16)
        dc_acc[...] += dot(dv[:, cols], state_low, 1, 1)
        db_acc[...] += dot(scaled[:, cols], adj_low, 1, 1)
        hi, low = halves(g_c * y_c - x_c * dx_c)
        sel = spread[0:heads, cols]
        dcum[...] += dot(sel, hi, 1, 1) + dot(sel, low, 1, 1)
        rows[3:4, cols] = jnp.sum(x_c * dx_state, 0, keepdims=True) + rows[0:1, cols] * jnp.sum(
            state * adj, 0, keepdims=True
        )
        return carry

    lax.fori_loop(0, chunks, finish, 0)

    gc_ref[...] = dc_acc[...].astype(BF16)
    gb_ref[...] = db_acc[...].astype(BF16)
    sums = jnp.concatenate([rows[3:5, :], jnp.zeros((14, feat), F32)], 0)
    hi, low = halves(sums)
    sel = spread[0:heads, :]
    per_head = dot(sel, hi, 1, 1) + dot(sel, low, 1, 1)
    lower_f = jnp.where(t_row >= t_col, 1.0, 0.0).astype(F32)
    dla = dot(dcum[...], lower_f, precision=lax.Precision.HIGHEST) + per_head[:, 0:1]
    gdt_ref[...] = -rate * dla
    alog_row = as_row(jnp.sum(dla * la, 1, keepdims=True))
    skip_row = as_row(per_head[:, 1:2])

    stores = [
        pltpu.make_async_copy(src, dst, store_sem.at[i])
        for i, (src, dst) in enumerate(
            [
                (y_ref, y_hbm),
                (gx_ref, gx_hbm),
                (gb_ref, gb_hbm),
                (gc_ref, gc_hbm),
                (gdt_ref, gdt_hbm),
            ]
        )
    ]
    for move in stores:
        move.start()
    red_seq[me] = jnp.zeros((8, LANES), F32)
    red_seq[me, 0:1, 0:heads] = alog_row
    red_seq[me, 1:2, 0:heads] = skip_row

    def share(axis, here, count, buf, send, recv):
        def copy(target, slot, o):
            return pltpu.make_async_remote_copy(
                src_ref=buf.at[here],
                dst_ref=buf.at[slot],
                send_sem=send.at[o],
                recv_sem=recv.at[slot],
                device_id={axis: target},
                device_id_type=MESH,
            )

        def go(o, carry):
            copy(lax.rem(here + o, count), here, o).start()
            return carry

        def come(o, carry):
            source = lax.rem(here + o, count)
            copy(source, source, o).wait_recv()
            copy(source, here, o).wait_send()
            return carry

        lax.fori_loop(1, count, go, 0)
        lax.fori_loop(1, count, come, 0)
        return jnp.sum(buf[...], 0)

    red_dp[mine] = share("seq", me, n_seq, red_seq, rs_send, rs_recv)
    total = share("dp", mine, n_dp, red_dp, rd_send, rd_recv)
    ga_ref[...] = total[0:1, 0:heads]
    gs_ref[...] = total[1:2, 0:heads]

    def drain(i, carry):
        c = i + odd * half
        away = i + (1 - odd) * half
        for d in range(2):
            lead, steps, _ = role(d)

            @pl.when(steps < pairs - 1)
            def _():
                p_copy(d, c).wait_send()

            @pl.when(jnp.logical_or(lead, steps > 0))
            def _():
                m_copy(d, c).wait_send()

            @pl.when(jnp.logical_or(lead, steps < pairs - 1))
            def _():
                l_copy(d, away).wait_send()

        return carry

    lax.fori_loop(0, half, drain, 0)
    for move in stores:
        move.wait()


def write_out(count, *refs):
    held = refs[2 * count : 3 * count]
    load, store = refs[3 * count :]
    loads = [pltpu.make_async_copy(refs[i], held[i], load.at[i]) for i in range(count)]
    stores = [
        pltpu.make_async_copy(held[i], refs[count + i], store.at[i]) for i in range(count)
    ]
    for copy in loads:
        copy.start()
    for first, second in zip(loads, stores):
        first.wait()
        second.start()
    for copy in stores:
        copy.wait()


def shards(n_seq, n_dp, x_in, b_in, c_in, dt, a_log, skip, cotangent):
    _, span, feat = x_in.shape
    state_dim = b_in.shape[2]
    heads = a_log.shape[0]
    width = 256
    chunks = feat // width
    blocks = (2, chunks, state_dim, width)
    vmem = pl.BlockSpec(memory_space=pltpu.VMEM)
    hbm = pl.BlockSpec(memory_space=pltpu.HBM)
    dma = pltpu.SemaphoreType.DMA
    wide = pltpu.VMEM((span, feat), F32)
    wide_low = pltpu.VMEM((span, feat), BF16)
    outs = pl.pallas_call(
        functools.partial(kernel, n_seq, n_dp, width),
        out_shape=(
            jax.ShapeDtypeStruct((span, feat), BF16),
            jax.ShapeDtypeStruct((span, feat), BF16),
            jax.ShapeDtypeStruct((span, state_dim), BF16),
            jax.ShapeDtypeStruct((span, state_dim), BF16),
            jax.ShapeDtypeStruct((heads, span), F32),
            jax.ShapeDtypeStruct((1, heads), F32),
            jax.ShapeDtypeStruct((1, heads), F32),
        ),
        in_specs=[hbm] * 7,
        out_specs=(hbm,) * 5 + (vmem,) * 2,
        scratch_shapes=[
            wide_low,
            wide_low,
            pltpu.VMEM((span, state_dim), BF16),
            pltpu.VMEM((span, state_dim), BF16),
            pltpu.VMEM((heads, span), F32),
            wide_low,
            pltpu.VMEM((span, state_dim), BF16),
            pltpu.VMEM((span, state_dim), BF16),
            pltpu.VMEM((heads, span), F32),
            pltpu.VMEM((1, heads), F32),
            pltpu.VMEM((1, heads), F32),
            wide_low,
            pltpu.VMEM((LANES, feat), BF16),
            pltpu.VMEM((LANES, span), F32),
            pltpu.VMEM((span, LANES), BF16),
            wide,
            wide,
            wide_low,
            wide_low,
            pltpu.VMEM((state_dim, span), BF16),
            pltpu.VMEM((state_dim, span), BF16),
            pltpu.VMEM(blocks, F32),
            pltpu.VMEM(blocks, F32),
            pltpu.VMEM(blocks, F32),
            pltpu.VMEM(blocks, F32),
            pltpu.VMEM(blocks, F32),
            pltpu.VMEM(blocks, F32),
            pltpu.VMEM((8, feat), F32),
            wide,
            wide,
            pltpu.VMEM((span, span), F32),
            pltpu.VMEM((span, span), F32),
            pltpu.VMEM((span, state_dim), F32),
            pltpu.VMEM((span, state_dim), F32),
            pltpu.VMEM((heads, span), F32),
            pltpu.VMEM((16, LANES), F32),
            pltpu.VMEM((16, LANES), F32),
            pltpu.VMEM((n_seq, 8, LANES), F32),
            pltpu.VMEM((n_dp, 8, LANES), F32),
            dma((2, chunks)),
            dma((2, chunks)),
            dma((2, chunks)),
            dma((2, chunks)),
            dma((2, chunks)),
            dma((2, chunks)),
            dma((2,)),
            dma((7,)),
            dma((5,)),
            dma((n_seq,)),
            dma((n_seq,)),
            dma((n_dp,)),
            dma((n_dp,)),
        ],
        compiler_params=pltpu.CompilerParams(
            collective_id=0, has_side_effects=True, vmem_limit_bytes=VMEM_BYTES
        ),
    )(x_in[0], b_in[0], c_in[0], dt[0], a_log[None], skip[None], cotangent[0])
    y, gx, gb, gc, gdt, ga, gs = pl.pallas_call(
        functools.partial(write_out, len(outs)),
        out_shape=tuple(jax.ShapeDtypeStruct(o.shape, o.dtype) for o in outs),
        in_specs=[hbm] * len(outs),
        out_specs=(hbm,) * len(outs),
        scratch_shapes=[pltpu.VMEM(o.shape, o.dtype) for o in outs]
        + [dma((len(outs),)), dma((len(outs),))],
        compiler_params=pltpu.CompilerParams(vmem_limit_bytes=VMEM_BYTES),
    )(*outs)
    return (y[None], gx[None], gb[None], gc[None], gdt[None], ga[0], gs[0])


def solution(mesh):
    tokens = P("dp", "seq", None)
    steps = P("dp", None, "seq")
    return jax.shard_map(
        functools.partial(shards, mesh.shape["seq"], mesh.shape["dp"]),
        mesh=mesh,
        in_specs=(tokens, tokens, tokens, steps, P(), P(), tokens),
        out_specs=(tokens, tokens, tokens, tokens, steps, P(), P()),
        check_vma=False,
    )
```

```python
import functools

import jax
import jax.numpy as jnp
from jax import lax
from jax.experimental import pallas as pl
from jax.experimental.pallas import tpu as pltpu
from jax.sharding import PartitionSpec as P

F32 = jnp.float32
BF16 = jnp.bfloat16
MESH = pl.DeviceIdType.MESH
LANES = 128
VMEM_BYTES = 62 * 1024 * 1024


def dot(a, b, ca=1, cb=0, precision=None):
    return lax.dot_general(
        a, b, (((ca,), (cb,)), ((), ())), preferred_element_type=F32, precision=precision
    )


def pack(v, heads):
    lane = lax.broadcasted_iota(jnp.int32, v.shape, 1)
    hi = v.astype(BF16).astype(F32)
    rest = v - hi
    mid = rest.astype(BF16).astype(F32)
    low = rest - mid
    out = jnp.where(lane < heads, hi, jnp.where(lane < 2 * heads, mid, low))
    return jnp.where(lane < 3 * heads, out, 0.0).astype(BF16)


def halves(v):
    hi = v.astype(BF16)
    return hi, (v - hi.astype(F32)).astype(BF16)


def kernel(
    n_seq,
    n_dp,
    width,
    x_hbm,
    b_hbm,
    c_hbm,
    dt_hbm,
    alog_hbm,
    skip_hbm,
    g_hbm,
    y_hbm,
    gx_hbm,
    gb_hbm,
    gc_hbm,
    gdt_hbm,
    ga_ref,
    gs_ref,
    y_ref,
    gx_ref,
    gb_ref,
    gc_ref,
    gdt_ref,
    x_ref,
    b_ref,
    c_ref,
    dt_ref,
    alog_ref,
    skip_ref,
    g_ref,
    spread,
    cum_rows,
    cum_pack,
    e_wide,
    to_wide,
    scaled,
    dv,
    bt,
    ct,
    local,
    p_in,
    p_out,
    other_local,
    entry,
    m_out,
    rows,
    y_acc,
    dx_acc,
    cb_ref,
    dcb,
    dc_acc,
    db_acc,
    dcum,
    sums,
    gain_own,
    gain_in,
    red_seq,
    red_dp,
    p_send,
    p_recv,
    m_send,
    m_recv,
    l_send,
    l_recv,
    g_sem,
    load_sem,
    store_sem,
    rs_send,
    rs_recv,
    rd_send,
    rd_recv,
):
    heads, span = dt_ref.shape
    feat = x_ref.shape[1]
    size = feat // heads
    chunks = feat // width
    pairs = n_seq // 2
    me = lax.axis_index("seq")
    mine = lax.axis_index("dp")
    place = me // 2
    odd = lax.rem(me, 2)
    partner = me + 1 - 2 * odd

    moves = [
        pltpu.make_async_copy(src, dst, load_sem.at[i])
        for i, (src, dst) in enumerate(
            [
                (dt_hbm, dt_ref),
                (alog_hbm, alog_ref),
                (skip_hbm, skip_ref),
                (b_hbm, b_ref),
                (c_hbm, c_ref),
                (x_hbm, x_ref),
                (g_hbm, g_ref),
            ]
        )
    ]
    for move in moves:
        move.start()
    barrier = pltpu.get_barrier_semaphore()

    def greet_seq(o, carry):
        pl.semaphore_signal(
            barrier, inc=1, device_id={"seq": lax.rem(me + o, n_seq)}, device_id_type=MESH
        )
        return carry

    def greet_dp(o, carry):
        pl.semaphore_signal(
            barrier, inc=1, device_id={"dp": lax.rem(mine + o, n_dp)}, device_id_type=MESH
        )
        return carry

    lax.fori_loop(1, n_seq, greet_seq, 0)
    lax.fori_loop(1, n_dp, greet_dp, 0)

    diag = lax.broadcasted_iota(jnp.int32, (heads, heads), 0) == lax.broadcasted_iota(
        jnp.int32, (heads, heads), 1
    )

    def column(row):
        return jnp.sum(jnp.where(diag, jnp.broadcast_to(row, (heads, heads)), 0.0), 1, keepdims=True)

    def as_row(col):
        return jnp.sum(jnp.where(diag, jnp.broadcast_to(col, (heads, heads)), 0.0), 0, keepdims=True)

    spread_row = lax.broadcasted_iota(jnp.int32, spread.shape, 0) & (heads - 1)
    spread_col = lax.shift_right_logical(
        lax.broadcasted_iota(jnp.int32, spread.shape, 1), size.bit_length() - 1
    )
    spread[...] = jnp.where(spread_row == spread_col, 1.0, 0.0).astype(BF16)
    for move in moves[:3]:
        move.wait()
    rate = jnp.exp(column(alog_ref[...]))
    la = -rate * dt_ref[...]
    t_row = lax.broadcasted_iota(jnp.int32, (span, span), 0)
    t_col = lax.broadcasted_iota(jnp.int32, (span, span), 1)
    upper = jnp.where(t_row <= t_col, 1.0, 0.0).astype(F32)
    cum = dot(jnp.concatenate([la] * (LANES // heads), 0), upper, precision=lax.Precision.HIGHEST)
    cum_rows[...] = cum
    cum_t = jnp.transpose(cum)
    cum_pack[...] = pack(cum_t, heads)
    e_t = jnp.exp(cum_t)
    gain_own[...] = e_t[span - 16 :, :]
    pl.semaphore_wait(barrier, n_seq - 1 + n_dp - 1)
    gain_copy = pltpu.make_async_remote_copy(
        src_ref=gain_own,
        dst_ref=gain_in,
        send_sem=g_sem.at[0],
        recv_sem=g_sem.at[1],
        device_id={"seq": partner},
        device_id_type=MESH,
    )
    gain_copy.start()

    e_pack = pack(e_t, heads)
    to_pack = pack(jnp.exp(cum_t[span - 1 :, :] - cum_t), heads)
    for move in moves[3:]:
        move.wait()
    bt[...] = jnp.transpose(b_ref[...].astype(F32)).astype(BF16)
    ct[...] = jnp.transpose(c_ref[...].astype(F32)).astype(BF16)
    skip_col = jnp.broadcast_to(column(skip_ref[...]), (heads, LANES))
    skip_pack = pack(jnp.transpose(jnp.concatenate([skip_col] * (LANES // heads), 0)), heads)

    def part(c):
        return pl.ds(pl.multiple_of(c * width, width), width)

    def role(d):
        lead = odd == d
        steps = jnp.where(d == 0, place, pairs - 1 - place)
        lead_row = jnp.broadcast_to(jnp.where(lead, 1, 0), (1, width)) == 1
        return lead, steps, lead_row

    def p_copy(d, c):
        return pltpu.make_async_remote_copy(
            src_ref=p_out.at[d, c],
            dst_ref=p_in.at[d, c],
            send_sem=p_send.at[d, c],
            recv_sem=p_recv.at[d, c],
            device_id={"seq": lax.rem(me + 2 - 4 * d + n_seq, n_seq)},
            device_id_type=MESH,
        )

    def m_copy(d, c):
        return pltpu.make_async_remote_copy(
            src_ref=m_out.at[d, c],
            dst_ref=entry.at[d, c],
            send_sem=m_send.at[d, c],
            recv_sem=m_recv.at[d, c],
            device_id={"seq": partner},
            device_id_type=MESH,
        )

    def l_copy(d, c):
        return pltpu.make_async_remote_copy(
            src_ref=local.at[d, c],
            dst_ref=other_local.at[d, c],
            send_sem=l_send.at[d, c],
            recv_sem=l_recv.at[d, c],
            device_id={"seq": partner},
            device_id_type=MESH,
        )

    half = chunks // 2
    blank = jnp.zeros((LANES, width), F32)

    def step(d, c):
        lead, steps, lead_row = role(d)
        cols = part(c)
        own = rows[0:1, cols]
        other = rows[1:2, cols]
        wanted = jnp.logical_or(jnp.logical_not(lead), steps < pairs - 1)

        @pl.when(wanted)
        def _():
            l_copy(d, c).wait_recv()

        @pl.when(jnp.logical_not(wanted))
        def _():
            other_local[d, c] = blank

        @pl.when(steps > 0)
        def _():
            p_copy(d, c).wait_recv()

        @pl.when(steps == 0)
        def _():
            p_in[d, c] = blank

        before = p_in[d, c]
        here = local[d, c]
        there = other_local[d, c]

        @pl.when(steps < pairs - 1)
        def _():
            p_out[d, c] = own * other * before + jnp.where(
                lead_row, other * here + there, own * there + here
            )
            p_copy(d, c).start()

        m_out[d, c] = jnp.where(lead_row, own * before + here, before)

        @pl.when(jnp.logical_or(lead, steps > 0))
        def _():
            m_copy(d, c).start()

        entry[d, c] = jnp.where(lead_row, before, other * before + there)

    def prepare(i, carry):
        c = lax.rem(i + (1 - odd) * half, chunks)
        cols = part(c)
        spread_c = spread[:, cols]
        e_c = dot(e_pack, spread_c)
        to_c = dot(to_pack, spread_c)
        e_wide[:, cols] = e_c
        to_wide[:, cols] = to_c
        x_c = x_ref[:, cols].astype(F32)
        g_c = g_ref[:, cols].astype(F32)
        sc = (x_c * to_c).astype(BF16)
        dv_c = (g_c * e_c).astype(BF16)
        scaled[:, cols] = sc
        dv[:, cols] = dv_c
        local[0, c] = dot(bt[...], sc)
        local[1, c] = dot(ct[...], dv_c)
        rows[:, cols] = jnp.zeros((8, width), F32)
        rows[0:1, cols] = e_c[span - 1 :, :]
        rows[2:3, cols] = dot(skip_pack[0:16], spread_c)[0:1]
        rows[4:5, cols] = jnp.sum(x_c * g_c, 0, keepdims=True)

        for d in range(2):
            lead, steps, _ = role(d)
            wanted = jnp.logical_or(lead, steps < pairs - 1)

            @pl.when(jnp.logical_and(i < half, wanted))
            def _():
                l_copy(d, c).start()

        return carry

    lax.fori_loop(0, chunks, prepare, 0)
    cb_ref[...] = dot(c_ref[...], b_ref[...], 1, 1)
    dcb[...] = jnp.zeros_like(dcb)
    sums[...] = jnp.zeros_like(sums)
    dcum[...] = jnp.zeros_like(dcum)
    gain_copy.wait()
    gain_pack = pack(gain_in[...], heads)
    rows[1:2, :] = dot(gain_pack, spread[...])[15:16, :]


    def inner(j, carry):
        cols = pl.ds(pl.multiple_of(j * 2 * size, 2 * size), 2 * size)
        x2 = x_ref[:, cols]
        g2 = g_ref[:, cols]
        lane = lax.broadcasted_iota(jnp.int32, (span, 2 * size), 1)
        lower = t_row >= t_col
        y2, dx2 = [], []
        total = dcb[...]
        for i in range(2):
            h = 2 * j + i
            pick_row = lax.broadcasted_iota(jnp.int32, (LANES, span), 0)
            pick = jnp.where((pick_row & (heads - 1)) == h, 1.0, 0.0).astype(BF16)
            at_t = dot(cum_pack[...], pick)
            decay = jnp.exp(jnp.where(lower, at_t - cum_rows[pl.ds(h, 1), :], -1e30))
            weights = (cb_ref[...] * decay).astype(BF16)
            y2.append(dot(weights, x2))
            dx2.append(dot(weights, g2, 0, 0))
            own_lanes = (lane < size) if i == 0 else (lane >= size)
            g_own = jnp.where(own_lanes, g2.astype(F32), 0.0).astype(BF16)
            total = total + dot(g_own, x2, 1, 1) * decay
        dcb[...] = total
        y_acc[:, cols] = jnp.where(lane < size, y2[0], y2[1])
        dx_acc[:, cols] = jnp.where(lane < size, dx2[0], dx2[1])
        return carry

    per_chunk = width // (2 * size)
    upper_half = jnp.where(place >= pairs // 2, 1, 0)

    def middle(i, carry):
        late = i // half
        step(upper_half + late - 2 * late * upper_half, lax.rem(i, half) + odd * half)
        return lax.fori_loop(i * per_chunk, (i + 1) * per_chunk, inner, carry)

    lax.fori_loop(0, chunks, middle, 0)

    dcb_low = dcb[...]
    dc_acc[...] = dot(dcb_low.astype(BF16), b_ref[...])
    db_acc[...] = dot(jnp.transpose(dcb_low).astype(BF16), c_ref[...])

    def finish(i, carry):
        c = lax.rem(i + odd * half, chunks)
        cols = part(c)
        for d in range(2):
            lead, steps, _ = role(d)
            nothing = jnp.logical_and(lead, steps == 0)

            @pl.when(jnp.logical_and(i >= half, nothing))
            def _():
                entry[d, c] = blank

            @pl.when(jnp.logical_and(i >= half, jnp.logical_not(nothing)))
            def _():
                m_copy(d, c).wait_recv()

        state = entry[0, c]
        adj = entry[1, c]
        state_low = state.astype(BF16)
        adj_low = adj.astype(BF16)
        x_c = x_ref[:, cols].astype(F32)
        g_c = g_ref[:, cols].astype(F32)
        skip_c = rows[2:3, cols]
        y_c = y_acc[:, cols] + e_wide[:, cols] * dot(c_ref[...], state_low)
        y_ref[:, cols] = (y_c + skip_c * x_c).astype(BF16)
        dx_state = to_wide[:, cols] * dot(b_ref[...], adj_low)
        dx_c = dx_acc[:, cols] + dx_state
        gx_ref[:, cols] = (dx_c + skip_c * g_c).astype(BF16)
        dc_acc[...] += dot(dv[:, cols], state_low, 1, 1)
        db_acc[...] += dot(scaled[:, cols], adj_low, 1, 1)
        hi, low = halves(g_c * y_c - x_c * dx_c)
        sel = spread[0:heads, cols]
        dcum[...] += dot(sel, hi, 1, 1) + dot(sel, low, 1, 1)
        rows[3:4, cols] = jnp.sum(x_c * dx_state, 0, keepdims=True) + rows[0:1, cols] * jnp.sum(
            state * adj, 0, keepdims=True
        )
        hi, low = halves(jnp.concatenate([rows[:, cols], jnp.zeros((8, width), F32)], 0))
        sums[...] += dot(sel, hi, 1, 1) + dot(sel, low, 1, 1)
        return carry

    lax.fori_loop(0, chunks, finish, 0)

    per_head = sums[...]
    last = per_head[:, 3:4]
    alog = jnp.sum(dcum[...] * cum_rows[0:heads, :], 1, keepdims=True)
    alog_row = as_row(alog + last * cum_rows[0:heads, span - 1 : span])
    red_seq[me] = jnp.zeros((8, LANES), F32)
    red_seq[me, 0:1, 0:heads] = alog_row
    red_seq[me, 1:2, 0:heads] = as_row(per_head[:, 4:5])

    def share(axis, here, count, buf, send, recv, between):
        def copy(target, slot, o):
            return pltpu.make_async_remote_copy(
                src_ref=buf.at[here],
                dst_ref=buf.at[slot],
                send_sem=send.at[o],
                recv_sem=recv.at[slot],
                device_id={axis: target},
                device_id_type=MESH,
            )

        def go(o, carry):
            copy(lax.rem(here + o, count), here, o).start()
            return carry

        def come(o, carry):
            source = lax.rem(here + o, count)
            copy(source, source, o).wait_recv()
            copy(source, here, o).wait_send()
            return carry

        lax.fori_loop(1, count, go, 0)
        between()
        lax.fori_loop(1, count, come, 0)
        return jnp.sum(buf[...], 0)

    stores = [
        pltpu.make_async_copy(src, dst, store_sem.at[i])
        for i, (src, dst) in enumerate(
            [
                (y_ref, y_hbm),
                (gx_ref, gx_hbm),
                (gb_ref, gb_hbm),
                (gc_ref, gc_hbm),
                (gdt_ref, gdt_hbm),
            ]
        )
    ]

    def meanwhile():
        stores[0].start()
        stores[1].start()
        gc_ref[...] = dc_acc[...].astype(BF16)
        gb_ref[...] = db_acc[...].astype(BF16)
        stores[2].start()
        stores[3].start()
        lower_f = jnp.where(t_row >= t_col, 1.0, 0.0).astype(F32)
        dla = dot(dcum[...], lower_f, precision=lax.Precision.HIGHEST) + last
        gdt_ref[...] = -rate * dla
        stores[4].start()

    red_dp[mine] = share("seq", me, n_seq, red_seq, rs_send, rs_recv, meanwhile)
    total = share("dp", mine, n_dp, red_dp, rd_send, rd_recv, lambda: None)
    ga_ref[...] = total[0:1, 0:heads]
    gs_ref[...] = total[1:2, 0:heads]

    def drain(i, carry):
        c = i + odd * half
        away = i + (1 - odd) * half
        for d in range(2):
            lead, steps, _ = role(d)

            @pl.when(steps < pairs - 1)
            def _():
                p_copy(d, c).wait_send()

            @pl.when(jnp.logical_or(lead, steps > 0))
            def _():
                m_copy(d, c).wait_send()

            @pl.when(jnp.logical_or(lead, steps < pairs - 1))
            def _():
                l_copy(d, away).wait_send()

        return carry

    lax.fori_loop(0, half, drain, 0)
    for move in stores:
        move.wait()


def write_out(count, pieces, *refs):
    held = refs[2 * count : 3 * count]
    load, store = refs[3 * count :]
    moves = []
    for i in range(count):
        cuts = pieces if i < 2 else 1
        size = held[i].shape[0] // cuts
        for k in range(cuts):
            at = pl.ds(k * size, size)
            n = len(moves)
            moves.append(
                (
                    pltpu.make_async_copy(refs[i].at[at], held[i].at[at], load.at[n]),
                    pltpu.make_async_copy(held[i].at[at], refs[count + i].at[at], store.at[n]),
                )
            )
    for first, _ in moves:
        first.start()
    for first, second in moves:
        first.wait()
        second.start()
    for _, second in moves:
        second.wait()


def shards(n_seq, n_dp, x_in, b_in, c_in, dt, a_log, skip, cotangent):
    _, span, feat = x_in.shape
    state_dim = b_in.shape[2]
    heads = a_log.shape[0]
    width = 256
    chunks = feat // width
    blocks = (2, chunks, state_dim, width)
    vmem = pl.BlockSpec(memory_space=pltpu.VMEM)
    hbm = pl.BlockSpec(memory_space=pltpu.HBM)
    dma = pltpu.SemaphoreType.DMA
    wide = pltpu.VMEM((span, feat), F32)
    wide_low = pltpu.VMEM((span, feat), BF16)
    outs = pl.pallas_call(
        functools.partial(kernel, n_seq, n_dp, width),
        out_shape=(
            jax.ShapeDtypeStruct((span, feat), BF16),
            jax.ShapeDtypeStruct((span, feat), BF16),
            jax.ShapeDtypeStruct((span, state_dim), BF16),
            jax.ShapeDtypeStruct((span, state_dim), BF16),
            jax.ShapeDtypeStruct((heads, span), F32),
            jax.ShapeDtypeStruct((1, heads), F32),
            jax.ShapeDtypeStruct((1, heads), F32),
        ),
        in_specs=[hbm] * 7,
        out_specs=(hbm,) * 5 + (vmem,) * 2,
        scratch_shapes=[
            wide_low,
            wide_low,
            pltpu.VMEM((span, state_dim), BF16),
            pltpu.VMEM((span, state_dim), BF16),
            pltpu.VMEM((heads, span), F32),
            wide_low,
            pltpu.VMEM((span, state_dim), BF16),
            pltpu.VMEM((span, state_dim), BF16),
            pltpu.VMEM((heads, span), F32),
            pltpu.VMEM((1, heads), F32),
            pltpu.VMEM((1, heads), F32),
            wide_low,
            pltpu.VMEM((LANES, feat), BF16),
            pltpu.VMEM((LANES, span), F32),
            pltpu.VMEM((span, LANES), BF16),
            wide,
            wide,
            wide_low,
            wide_low,
            pltpu.VMEM((state_dim, span), BF16),
            pltpu.VMEM((state_dim, span), BF16),
            pltpu.VMEM(blocks, F32),
            pltpu.VMEM(blocks, F32),
            pltpu.VMEM(blocks, F32),
            pltpu.VMEM(blocks, F32),
            pltpu.VMEM(blocks, F32),
            pltpu.VMEM(blocks, F32),
            pltpu.VMEM((8, feat), F32),
            wide,
            wide,
            pltpu.VMEM((span, span), F32),
            pltpu.VMEM((span, span), F32),
            pltpu.VMEM((span, state_dim), F32),
            pltpu.VMEM((span, state_dim), F32),
            pltpu.VMEM((heads, span), F32),
            pltpu.VMEM((heads, 16), F32),
            pltpu.VMEM((16, LANES), F32),
            pltpu.VMEM((16, LANES), F32),
            pltpu.VMEM((n_seq, 8, LANES), F32),
            pltpu.VMEM((n_dp, 8, LANES), F32),
            dma((2, chunks)),
            dma((2, chunks)),
            dma((2, chunks)),
            dma((2, chunks)),
            dma((2, chunks)),
            dma((2, chunks)),
            dma((2,)),
            dma((7,)),
            dma((5,)),
            dma((n_seq,)),
            dma((n_seq,)),
            dma((n_dp,)),
            dma((n_dp,)),
        ],
        compiler_params=pltpu.CompilerParams(
            collective_id=0, has_side_effects=True, vmem_limit_bytes=VMEM_BYTES
        ),
    )(x_in[0], b_in[0], c_in[0], dt[0], a_log[None], skip[None], cotangent[0])
    y, gx, gb, gc, gdt, ga, gs = pl.pallas_call(
        functools.partial(write_out, len(outs), 4),
        out_shape=tuple(jax.ShapeDtypeStruct(o.shape, o.dtype) for o in outs),
        in_specs=[hbm] * len(outs),
        out_specs=(hbm,) * len(outs),
        scratch_shapes=[pltpu.VMEM(o.shape, o.dtype) for o in outs]
        + [dma((len(outs) + 6,)), dma((len(outs) + 6,))],
        compiler_params=pltpu.CompilerParams(vmem_limit_bytes=VMEM_BYTES),
    )(*outs)
    return (y[None], gx[None], gb[None], gc[None], gdt[None], ga[0], gs[0])


def solution(mesh):
    tokens = P("dp", "seq", None)
    steps = P("dp", None, "seq")
    return jax.shard_map(
        functools.partial(shards, mesh.shape["seq"], mesh.shape["dp"]),
        mesh=mesh,
        in_specs=(tokens, tokens, tokens, steps, P(), P(), tokens),
        out_specs=(tokens, tokens, tokens, tokens, steps, P(), P()),
        check_vma=False,
    )
```

```python
import functools

import jax
import jax.numpy as jnp
from jax import lax
from jax.experimental import pallas as pl
from jax.experimental.pallas import tpu as pltpu
from jax.sharding import PartitionSpec as P

F32 = jnp.float32
BF16 = jnp.bfloat16
MESH = pl.DeviceIdType.MESH
LANES = 128
VMEM_BYTES = 62 * 1024 * 1024


def dot(a, b, ca=1, cb=0, precision=None):
    return lax.dot_general(
        a, b, (((ca,), (cb,)), ((), ())), preferred_element_type=F32, precision=precision
    )


def pack(v, heads):
    lane = lax.broadcasted_iota(jnp.int32, v.shape, 1)
    hi = v.astype(BF16).astype(F32)
    rest = v - hi
    mid = rest.astype(BF16).astype(F32)
    low = rest - mid
    out = jnp.where(lane < heads, hi, jnp.where(lane < 2 * heads, mid, low))
    return jnp.where(lane < 3 * heads, out, 0.0).astype(BF16)


def halves(v):
    hi = v.astype(BF16)
    return hi, (v - hi.astype(F32)).astype(BF16)


def kernel(
    n_seq,
    n_dp,
    width,
    x_hbm,
    b_hbm,
    c_hbm,
    dt_hbm,
    alog_hbm,
    skip_hbm,
    g_hbm,
    y_hbm,
    gx_hbm,
    gb_hbm,
    gc_hbm,
    gdt_hbm,
    ga_ref,
    gs_ref,
    y_ref,
    gx_ref,
    gb_ref,
    gc_ref,
    gdt_ref,
    x_ref,
    b_ref,
    c_ref,
    dt_ref,
    alog_ref,
    skip_ref,
    g_ref,
    spread,
    cum_rows,
    cum_pack,
    e_wide,
    to_wide,
    scaled,
    dv,
    bt,
    ct,
    local,
    p_in,
    p_out,
    other_local,
    entry,
    m_out,
    rows,
    y_acc,
    dx_acc,
    cb_ref,
    dcb,
    dc_acc,
    db_acc,
    dcum,
    sums,
    gain_own,
    gain_in,
    red_seq,
    red_dp,
    p_send,
    p_recv,
    m_send,
    m_recv,
    l_send,
    l_recv,
    g_sem,
    load_sem,
    store_sem,
    rs_send,
    rs_recv,
    rd_send,
    rd_recv,
):
    heads, span = dt_ref.shape
    feat = x_ref.shape[1]
    size = feat // heads
    chunks = feat // width
    pairs = n_seq // 2
    me = lax.axis_index("seq")
    mine = lax.axis_index("dp")
    place = me // 2
    odd = lax.rem(me, 2)
    partner = me + 1 - 2 * odd

    moves = [
        pltpu.make_async_copy(src, dst, load_sem.at[i])
        for i, (src, dst) in enumerate(
            [
                (dt_hbm, dt_ref),
                (alog_hbm, alog_ref),
                (skip_hbm, skip_ref),
                (b_hbm, b_ref),
                (c_hbm, c_ref),
                (x_hbm, x_ref),
                (g_hbm, g_ref),
            ]
        )
    ]
    for move in moves:
        move.start()
    barrier = pltpu.get_barrier_semaphore()

    def greet_seq(o, carry):
        pl.semaphore_signal(
            barrier, inc=1, device_id={"seq": lax.rem(me + o, n_seq)}, device_id_type=MESH
        )
        return carry

    def greet_dp(o, carry):
        pl.semaphore_signal(
            barrier, inc=1, device_id={"dp": lax.rem(mine + o, n_dp)}, device_id_type=MESH
        )
        return carry

    lax.fori_loop(1, n_seq, greet_seq, 0)
    lax.fori_loop(1, n_dp, greet_dp, 0)

    diag = lax.broadcasted_iota(jnp.int32, (heads, heads), 0) == lax.broadcasted_iota(
        jnp.int32, (heads, heads), 1
    )

    def column(row):
        return jnp.sum(jnp.where(diag, jnp.broadcast_to(row, (heads, heads)), 0.0), 1, keepdims=True)

    def as_row(col):
        return jnp.sum(jnp.where(diag, jnp.broadcast_to(col, (heads, heads)), 0.0), 0, keepdims=True)

    spread_row = lax.broadcasted_iota(jnp.int32, spread.shape, 0) & (heads - 1)
    spread_col = lax.shift_right_logical(
        lax.broadcasted_iota(jnp.int32, spread.shape, 1), size.bit_length() - 1
    )
    spread[...] = jnp.where(spread_row == spread_col, 1.0, 0.0).astype(BF16)
    for move in moves[:3]:
        move.wait()
    rate = jnp.exp(column(alog_ref[...]))
    la = -rate * dt_ref[...]
    t_row = lax.broadcasted_iota(jnp.int32, (span, span), 0)
    t_col = lax.broadcasted_iota(jnp.int32, (span, span), 1)
    upper = jnp.where(t_row <= t_col, 1.0, 0.0).astype(F32)
    cum = dot(jnp.concatenate([la] * (LANES // heads), 0), upper, precision=lax.Precision.HIGHEST)
    cum_rows[...] = cum
    cum_t = jnp.transpose(cum)
    cum_pack[...] = pack(cum_t, heads)
    e_t = jnp.exp(cum_t)
    gain_own[...] = e_t[span - 16 :, :]
    pl.semaphore_wait(barrier, n_seq - 1 + n_dp - 1)
    gain_copy = pltpu.make_async_remote_copy(
        src_ref=gain_own,
        dst_ref=gain_in,
        send_sem=g_sem.at[0],
        recv_sem=g_sem.at[1],
        device_id={"seq": partner},
        device_id_type=MESH,
    )
    gain_copy.start()

    e_pack = pack(e_t, heads)
    to_pack = pack(jnp.exp(cum_t[span - 1 :, :] - cum_t), heads)
    for move in moves[3:]:
        move.wait()
    bt[...] = jnp.transpose(b_ref[...].astype(F32)).astype(BF16)
    ct[...] = jnp.transpose(c_ref[...].astype(F32)).astype(BF16)
    skip_col = jnp.broadcast_to(column(skip_ref[...]), (heads, LANES))
    skip_pack = pack(jnp.transpose(jnp.concatenate([skip_col] * (LANES // heads), 0)), heads)

    def part(c):
        return pl.ds(pl.multiple_of(c * width, width), width)

    def role(d):
        lead = odd == d
        steps = jnp.where(d == 0, place, pairs - 1 - place)
        lead_row = jnp.broadcast_to(jnp.where(lead, 1, 0), (1, width)) == 1
        return lead, steps, lead_row

    def p_copy(d, c):
        return pltpu.make_async_remote_copy(
            src_ref=p_out.at[d, c],
            dst_ref=p_in.at[d, c],
            send_sem=p_send.at[d, c],
            recv_sem=p_recv.at[d, c],
            device_id={"seq": lax.rem(me + 2 - 4 * d + n_seq, n_seq)},
            device_id_type=MESH,
        )

    def m_copy(d, c):
        return pltpu.make_async_remote_copy(
            src_ref=m_out.at[d, c],
            dst_ref=entry.at[d, c],
            send_sem=m_send.at[d, c],
            recv_sem=m_recv.at[d, c],
            device_id={"seq": partner},
            device_id_type=MESH,
        )

    def l_copy(d, c):
        return pltpu.make_async_remote_copy(
            src_ref=local.at[d, c],
            dst_ref=other_local.at[d, c],
            send_sem=l_send.at[d, c],
            recv_sem=l_recv.at[d, c],
            device_id={"seq": partner},
            device_id_type=MESH,
        )

    half = chunks // 2
    blank = jnp.zeros((LANES, width), F32)

    def step(d, c):
        lead, steps, lead_row = role(d)
        cols = part(c)
        own = rows[0:1, cols]
        other = rows[1:2, cols]
        wanted = jnp.logical_or(jnp.logical_not(lead), steps < pairs - 1)

        @pl.when(wanted)
        def _():
            l_copy(d, c).wait_recv()

        @pl.when(jnp.logical_not(wanted))
        def _():
            other_local[d, c] = blank

        @pl.when(steps > 0)
        def _():
            p_copy(d, c).wait_recv()

        @pl.when(steps == 0)
        def _():
            p_in[d, c] = blank

        before = p_in[d, c]
        here = local[d, c]
        there = other_local[d, c]

        @pl.when(steps < pairs - 1)
        def _():
            p_out[d, c] = own * other * before + jnp.where(
                lead_row, other * here + there, own * there + here
            )
            p_copy(d, c).start()

        m_out[d, c] = jnp.where(lead_row, own * before + here, before)

        @pl.when(jnp.logical_or(lead, steps > 0))
        def _():
            m_copy(d, c).start()

        entry[d, c] = jnp.where(lead_row, before, other * before + there)

    def prepare(i, carry):
        c = lax.rem(i + (1 - odd) * half, chunks)
        cols = part(c)
        spread_c = spread[:, cols]
        e_c = dot(e_pack, spread_c)
        to_c = dot(to_pack, spread_c)
        e_wide[:, cols] = e_c
        to_wide[:, cols] = to_c
        x_c = x_ref[:, cols].astype(F32)
        g_c = g_ref[:, cols].astype(F32)
        sc = (x_c * to_c).astype(BF16)
        dv_c = (g_c * e_c).astype(BF16)
        scaled[:, cols] = sc
        dv[:, cols] = dv_c
        local[0, c] = dot(bt[...], sc)
        local[1, c] = dot(ct[...], dv_c)
        rows[:, cols] = jnp.zeros((8, width), F32)
        rows[0:1, cols] = e_c[span - 1 :, :]
        rows[2:3, cols] = dot(skip_pack[0:16], spread_c)[0:1]
        rows[4:5, cols] = jnp.sum(x_c * g_c, 0, keepdims=True)

        for d in range(2):
            lead, steps, _ = role(d)
            wanted = jnp.logical_or(lead, steps < pairs - 1)

            @pl.when(jnp.logical_and(i < half, wanted))
            def _():
                l_copy(d, c).start()

        return carry

    lax.fori_loop(0, chunks, prepare, 0)
    cb_ref[...] = dot(c_ref[...], b_ref[...], 1, 1)
    dcb[...] = jnp.zeros_like(dcb)
    sums[...] = jnp.zeros_like(sums)
    dcum[...] = jnp.zeros_like(dcum)
    gain_copy.wait()
    gain_pack = pack(gain_in[...], heads)
    rows[1:2, :] = dot(gain_pack, spread[...])[15:16, :]


    mid = span // 2
    low_part, high_part = slice(0, mid), slice(mid, span)
    lane = lax.broadcasted_iota(jnp.int32, (span, 2 * size), 1)
    lower = lax.broadcasted_iota(jnp.int32, (mid, mid), 0) >= lax.broadcasted_iota(
        jnp.int32, (mid, mid), 1
    )
    pick_row = lax.broadcasted_iota(jnp.int32, (LANES, mid), 0) & (heads - 1)

    def inner(j):
        cols = pl.ds(pl.multiple_of(j * 2 * size, 2 * size), 2 * size)
        x2 = x_ref[:, cols]
        g2 = g_ref[:, cols]
        y2, dx2 = [], []
        t00, t1 = 0.0, 0.0
        for i in range(2):
            h = 2 * j + i
            pick = jnp.where(pick_row == h, 1.0, 0.0).astype(BF16)
            at_t = dot(cum_pack[...], pick)
            row = cum_rows[pl.ds(h, 1), :]
            at_low, at_high = at_t[low_part], at_t[high_part]
            d00 = jnp.exp(jnp.where(lower, at_low - row[:, low_part], -1e30))
            d10 = jnp.exp(at_high - row[:, low_part])
            d11 = jnp.exp(jnp.where(lower, at_high - row[:, high_part], -1e30))
            d1 = jnp.concatenate([d10, d11], 1)
            w00 = (cb_ref[low_part, low_part] * d00).astype(BF16)
            w1 = (cb_ref[high_part, :] * d1).astype(BF16)
            y2.append(jnp.concatenate([dot(w00, x2[low_part]), dot(w1, x2)], 0))
            left = jnp.concatenate([w00, w1[:, low_part]], 0)
            dx2.append(
                jnp.concatenate([dot(left, g2, 0, 0), dot(w1[:, high_part], g2[high_part], 0, 0)], 0)
            )
            own_lanes = (lane < size) if i == 0 else (lane >= size)
            g_own = jnp.where(own_lanes, g2.astype(F32), 0.0).astype(BF16)
            t00 = t00 + dot(g_own[low_part], x2[low_part], 1, 1) * d00
            t1 = t1 + dot(g_own[high_part], x2, 1, 1) * d1
        dcb[low_part, low_part] += t00
        dcb[high_part, :] += t1
        y_acc[:, cols] = jnp.where(lane < size, y2[0], y2[1])
        dx_acc[:, cols] = jnp.where(lane < size, dx2[0], dx2[1])

    per_chunk = width // (2 * size)
    upper_half = jnp.where(place >= pairs // 2, 1, 0)

    def middle(i, carry):
        late = i // half
        step(upper_half + late - 2 * late * upper_half, lax.rem(i, half) + odd * half)
        for k in range(per_chunk):
            inner(i * per_chunk + k)
        return carry

    lax.fori_loop(0, chunks, middle, 0)

    dcb_low = dcb[...]
    dc_acc[...] = dot(dcb_low.astype(BF16), b_ref[...])
    db_acc[...] = dot(jnp.transpose(dcb_low).astype(BF16), c_ref[...])

    def finish(i, carry):
        c = lax.rem(i + odd * half, chunks)
        cols = part(c)
        for d in range(2):
            lead, steps, _ = role(d)
            nothing = jnp.logical_and(lead, steps == 0)

            @pl.when(jnp.logical_and(i >= half, nothing))
            def _():
                entry[d, c] = blank

            @pl.when(jnp.logical_and(i >= half, jnp.logical_not(nothing)))
            def _():
                m_copy(d, c).wait_recv()

        state = entry[0, c]
        adj = entry[1, c]
        state_low = state.astype(BF16)
        adj_low = adj.astype(BF16)
        x_c = x_ref[:, cols].astype(F32)
        g_c = g_ref[:, cols].astype(F32)
        skip_c = rows[2:3, cols]
        y_c = y_acc[:, cols] + e_wide[:, cols] * dot(c_ref[...], state_low)
        y_ref[:, cols] = (y_c + skip_c * x_c).astype(BF16)
        dx_state = to_wide[:, cols] * dot(b_ref[...], adj_low)
        dx_c = dx_acc[:, cols] + dx_state
        gx_ref[:, cols] = (dx_c + skip_c * g_c).astype(BF16)
        dc_acc[...] += dot(dv[:, cols], state_low, 1, 1)
        db_acc[...] += dot(scaled[:, cols], adj_low, 1, 1)
        hi, low = halves(g_c * y_c - x_c * dx_c)
        sel = spread[0:heads, cols]
        dcum[...] += dot(sel, hi, 1, 1) + dot(sel, low, 1, 1)
        rows[3:4, cols] = jnp.sum(x_c * dx_state, 0, keepdims=True) + rows[0:1, cols] * jnp.sum(
            state * adj, 0, keepdims=True
        )
        hi, low = halves(jnp.concatenate([rows[:, cols], jnp.zeros((8, width), F32)], 0))
        sums[...] += dot(sel, hi, 1, 1) + dot(sel, low, 1, 1)
        return carry

    lax.fori_loop(0, chunks, finish, 0)

    per_head = sums[...]
    last = per_head[:, 3:4]
    alog = jnp.sum(dcum[...] * cum_rows[0:heads, :], 1, keepdims=True)
    alog_row = as_row(alog + last * cum_rows[0:heads, span - 1 : span])
    red_seq[me] = jnp.zeros((8, LANES), F32)
    red_seq[me, 0:1, 0:heads] = alog_row
    red_seq[me, 1:2, 0:heads] = as_row(per_head[:, 4:5])

    def share(axis, here, count, buf, send, recv, between):
        def copy(target, slot, o):
            return pltpu.make_async_remote_copy(
                src_ref=buf.at[here],
                dst_ref=buf.at[slot],
                send_sem=send.at[o],
                recv_sem=recv.at[slot],
                device_id={axis: target},
                device_id_type=MESH,
            )

        def go(o, carry):
            copy(lax.rem(here + o, count), here, o).start()
            return carry

        def come(o, carry):
            source = lax.rem(here + o, count)
            copy(source, source, o).wait_recv()
            copy(source, here, o).wait_send()
            return carry

        lax.fori_loop(1, count, go, 0)
        between()
        lax.fori_loop(1, count, come, 0)
        return jnp.sum(buf[...], 0)

    stores = [
        pltpu.make_async_copy(src, dst, store_sem.at[i])
        for i, (src, dst) in enumerate(
            [
                (y_ref, y_hbm),
                (gx_ref, gx_hbm),
                (gb_ref, gb_hbm),
                (gc_ref, gc_hbm),
                (gdt_ref, gdt_hbm),
            ]
        )
    ]

    def meanwhile():
        stores[0].start()
        stores[1].start()
        gc_ref[...] = dc_acc[...].astype(BF16)
        gb_ref[...] = db_acc[...].astype(BF16)
        stores[2].start()
        stores[3].start()
        lower_f = jnp.where(t_row >= t_col, 1.0, 0.0).astype(F32)
        dla = dot(dcum[...], lower_f, precision=lax.Precision.HIGHEST) + last
        gdt_ref[...] = -rate * dla
        stores[4].start()

    red_dp[mine] = share("seq", me, n_seq, red_seq, rs_send, rs_recv, meanwhile)
    total = share("dp", mine, n_dp, red_dp, rd_send, rd_recv, lambda: None)
    ga_ref[...] = total[0:1, 0:heads]
    gs_ref[...] = total[1:2, 0:heads]

    def drain(i, carry):
        c = i + odd * half
        away = i + (1 - odd) * half
        for d in range(2):
            lead, steps, _ = role(d)

            @pl.when(steps < pairs - 1)
            def _():
                p_copy(d, c).wait_send()

            @pl.when(jnp.logical_or(lead, steps > 0))
            def _():
                m_copy(d, c).wait_send()

            @pl.when(jnp.logical_or(lead, steps < pairs - 1))
            def _():
                l_copy(d, away).wait_send()

        return carry

    lax.fori_loop(0, half, drain, 0)
    for move in stores:
        move.wait()


def write_out(count, pieces, *refs):
    held = refs[2 * count : 3 * count]
    load, store = refs[3 * count :]
    moves = []
    for i in range(count):
        cuts = pieces if i < 2 else 1
        size = held[i].shape[0] // cuts
        for k in range(cuts):
            at = pl.ds(k * size, size)
            n = len(moves)
            moves.append(
                (
                    pltpu.make_async_copy(refs[i].at[at], held[i].at[at], load.at[n]),
                    pltpu.make_async_copy(held[i].at[at], refs[count + i].at[at], store.at[n]),
                )
            )
    for first, _ in moves:
        first.start()
    for first, second in moves:
        first.wait()
        second.start()
    for _, second in moves:
        second.wait()


def shards(n_seq, n_dp, x_in, b_in, c_in, dt, a_log, skip, cotangent):
    _, span, feat = x_in.shape
    state_dim = b_in.shape[2]
    heads = a_log.shape[0]
    width = 256
    chunks = feat // width
    blocks = (2, chunks, state_dim, width)
    vmem = pl.BlockSpec(memory_space=pltpu.VMEM)
    hbm = pl.BlockSpec(memory_space=pltpu.HBM)
    dma = pltpu.SemaphoreType.DMA
    wide = pltpu.VMEM((span, feat), F32)
    wide_low = pltpu.VMEM((span, feat), BF16)
    outs = pl.pallas_call(
        functools.partial(kernel, n_seq, n_dp, width),
        out_shape=(
            jax.ShapeDtypeStruct((span, feat), BF16),
            jax.ShapeDtypeStruct((span, feat), BF16),
            jax.ShapeDtypeStruct((span, state_dim), BF16),
            jax.ShapeDtypeStruct((span, state_dim), BF16),
            jax.ShapeDtypeStruct((heads, span), F32),
            jax.ShapeDtypeStruct((1, heads), F32),
            jax.ShapeDtypeStruct((1, heads), F32),
        ),
        in_specs=[hbm] * 7,
        out_specs=(hbm,) * 5 + (vmem,) * 2,
        scratch_shapes=[
            wide_low,
            wide_low,
            pltpu.VMEM((span, state_dim), BF16),
            pltpu.VMEM((span, state_dim), BF16),
            pltpu.VMEM((heads, span), F32),
            wide_low,
            pltpu.VMEM((span, state_dim), BF16),
            pltpu.VMEM((span, state_dim), BF16),
            pltpu.VMEM((heads, span), F32),
            pltpu.VMEM((1, heads), F32),
            pltpu.VMEM((1, heads), F32),
            wide_low,
            pltpu.VMEM((LANES, feat), BF16),
            pltpu.VMEM((LANES, span), F32),
            pltpu.VMEM((span, LANES), BF16),
            wide,
            wide,
            wide_low,
            wide_low,
            pltpu.VMEM((state_dim, span), BF16),
            pltpu.VMEM((state_dim, span), BF16),
            pltpu.VMEM(blocks, F32),
            pltpu.VMEM(blocks, F32),
            pltpu.VMEM(blocks, F32),
            pltpu.VMEM(blocks, F32),
            pltpu.VMEM(blocks, F32),
            pltpu.VMEM(blocks, F32),
            pltpu.VMEM((8, feat), F32),
            wide,
            wide,
            pltpu.VMEM((span, span), F32),
            pltpu.VMEM((span, span), F32),
            pltpu.VMEM((span, state_dim), F32),
            pltpu.VMEM((span, state_dim), F32),
            pltpu.VMEM((heads, span), F32),
            pltpu.VMEM((heads, 16), F32),
            pltpu.VMEM((16, LANES), F32),
            pltpu.VMEM((16, LANES), F32),
            pltpu.VMEM((n_seq, 8, LANES), F32),
            pltpu.VMEM((n_dp, 8, LANES), F32),
            dma((2, chunks)),
            dma((2, chunks)),
            dma((2, chunks)),
            dma((2, chunks)),
            dma((2, chunks)),
            dma((2, chunks)),
            dma((2,)),
            dma((7,)),
            dma((5,)),
            dma((n_seq,)),
            dma((n_seq,)),
            dma((n_dp,)),
            dma((n_dp,)),
        ],
        compiler_params=pltpu.CompilerParams(
            collective_id=0, has_side_effects=True, vmem_limit_bytes=VMEM_BYTES
        ),
    )(x_in[0], b_in[0], c_in[0], dt[0], a_log[None], skip[None], cotangent[0])
    y, gx, gb, gc, gdt, ga, gs = pl.pallas_call(
        functools.partial(write_out, len(outs), 4),
        out_shape=tuple(jax.ShapeDtypeStruct(o.shape, o.dtype) for o in outs),
        in_specs=[hbm] * len(outs),
        out_specs=(hbm,) * len(outs),
        scratch_shapes=[pltpu.VMEM(o.shape, o.dtype) for o in outs]
        + [dma((len(outs) + 6,)), dma((len(outs) + 6,))],
        compiler_params=pltpu.CompilerParams(vmem_limit_bytes=VMEM_BYTES),
    )(*outs)
    return (y[None], gx[None], gb[None], gc[None], gdt[None], ga[0], gs[0])


def solution(mesh):
    tokens = P("dp", "seq", None)
    steps = P("dp", None, "seq")
    return jax.shard_map(
        functools.partial(shards, mesh.shape["seq"], mesh.shape["dp"]),
        mesh=mesh,
        in_specs=(tokens, tokens, tokens, steps, P(), P(), tokens),
        out_specs=(tokens, tokens, tokens, tokens, steps, P(), P()),
        check_vma=False,
    )
```

```python
import functools

import jax
import jax.numpy as jnp
from jax import lax
from jax.experimental import pallas as pl
from jax.experimental.pallas import tpu as pltpu
from jax.sharding import PartitionSpec as P

F32 = jnp.float32
BF16 = jnp.bfloat16
MESH = pl.DeviceIdType.MESH
LANES = 128
VMEM_BYTES = 62 * 1024 * 1024


def dot(a, b, ca=1, cb=0, precision=None):
    return lax.dot_general(
        a, b, (((ca,), (cb,)), ((), ())), preferred_element_type=F32, precision=precision
    )


def pack(v, heads):
    lane = lax.broadcasted_iota(jnp.int32, v.shape, 1)
    hi = v.astype(BF16).astype(F32)
    rest = v - hi
    mid = rest.astype(BF16).astype(F32)
    low = rest - mid
    out = jnp.where(lane < heads, hi, jnp.where(lane < 2 * heads, mid, low))
    return jnp.where(lane < 3 * heads, out, 0.0).astype(BF16)


def halves(v):
    hi = v.astype(BF16)
    return hi, (v - hi.astype(F32)).astype(BF16)


def kernel(
    n_seq,
    n_dp,
    width,
    x_hbm,
    b_hbm,
    c_hbm,
    dt_hbm,
    alog_hbm,
    skip_hbm,
    g_hbm,
    y_hbm,
    gx_hbm,
    gb_hbm,
    gc_hbm,
    gdt_hbm,
    ga_ref,
    gs_ref,
    y_ref,
    gx_ref,
    gb_ref,
    gc_ref,
    gdt_ref,
    x_ref,
    b_ref,
    c_ref,
    dt_ref,
    alog_ref,
    skip_ref,
    g_ref,
    spread,
    cum_rows,
    cum_pack,
    e_wide,
    to_wide,
    scaled,
    dv,
    bt,
    ct,
    local,
    p_in,
    p_out,
    other_local,
    entry,
    m_out,
    relay,
    rows,
    y_acc,
    dx_acc,
    cb_ref,
    dcb,
    dc_acc,
    db_acc,
    dcum,
    sums,
    gain_own,
    gain_in,
    red_seq,
    red_dp,
    p_send,
    p_recv,
    m_send,
    m_recv,
    l_send,
    l_recv,
    r_send,
    r_recv,
    g_sem,
    load_sem,
    store_sem,
    rs_send,
    rs_recv,
    rd_send,
    rd_recv,
):
    heads, span = dt_ref.shape
    feat = x_ref.shape[1]
    size = feat // heads
    chunks = feat // width
    pairs = n_seq // 2
    me = lax.axis_index("seq")
    mine = lax.axis_index("dp")
    place = me // 2
    odd = lax.rem(me, 2)
    partner = me + 1 - 2 * odd

    moves = [
        pltpu.make_async_copy(src, dst, load_sem.at[i])
        for i, (src, dst) in enumerate(
            [
                (dt_hbm, dt_ref),
                (alog_hbm, alog_ref),
                (skip_hbm, skip_ref),
                (b_hbm, b_ref),
                (c_hbm, c_ref),
                (x_hbm, x_ref),
                (g_hbm, g_ref),
            ]
        )
    ]
    for move in moves:
        move.start()
    barrier = pltpu.get_barrier_semaphore()

    def greet_seq(o, carry):
        pl.semaphore_signal(
            barrier, inc=1, device_id={"seq": lax.rem(me + o, n_seq)}, device_id_type=MESH
        )
        return carry

    def greet_dp(o, carry):
        pl.semaphore_signal(
            barrier, inc=1, device_id={"dp": lax.rem(mine + o, n_dp)}, device_id_type=MESH
        )
        return carry

    lax.fori_loop(1, n_seq, greet_seq, 0)
    lax.fori_loop(1, n_dp, greet_dp, 0)

    diag = lax.broadcasted_iota(jnp.int32, (heads, heads), 0) == lax.broadcasted_iota(
        jnp.int32, (heads, heads), 1
    )

    def column(row):
        return jnp.sum(jnp.where(diag, jnp.broadcast_to(row, (heads, heads)), 0.0), 1, keepdims=True)

    def as_row(col):
        return jnp.sum(jnp.where(diag, jnp.broadcast_to(col, (heads, heads)), 0.0), 0, keepdims=True)

    spread_row = lax.broadcasted_iota(jnp.int32, spread.shape, 0) & (heads - 1)
    spread_col = lax.shift_right_logical(
        lax.broadcasted_iota(jnp.int32, spread.shape, 1), size.bit_length() - 1
    )
    spread[...] = jnp.where(spread_row == spread_col, 1.0, 0.0).astype(BF16)
    for move in moves[:3]:
        move.wait()
    rate = jnp.exp(column(alog_ref[...]))
    la = -rate * dt_ref[...]
    t_row = lax.broadcasted_iota(jnp.int32, (span, span), 0)
    t_col = lax.broadcasted_iota(jnp.int32, (span, span), 1)
    upper = jnp.where(t_row <= t_col, 1.0, 0.0).astype(F32)
    cum = dot(jnp.concatenate([la] * (LANES // heads), 0), upper, precision=lax.Precision.HIGHEST)
    cum_rows[...] = cum
    cum_t = jnp.transpose(cum)
    cum_pack[...] = pack(cum_t, heads)
    e_t = jnp.exp(cum_t)
    gain_own[...] = e_t[span - 16 :, :]
    pl.semaphore_wait(barrier, n_seq - 1 + n_dp - 1)
    gain_copy = pltpu.make_async_remote_copy(
        src_ref=gain_own,
        dst_ref=gain_in,
        send_sem=g_sem.at[0],
        recv_sem=g_sem.at[1],
        device_id={"seq": partner},
        device_id_type=MESH,
    )
    gain_copy.start()

    e_pack = pack(e_t, heads)
    to_pack = pack(jnp.exp(cum_t[span - 1 :, :] - cum_t), heads)
    for move in moves[3:]:
        move.wait()
    bt[...] = jnp.transpose(b_ref[...].astype(F32)).astype(BF16)
    ct[...] = jnp.transpose(c_ref[...].astype(F32)).astype(BF16)
    skip_col = jnp.broadcast_to(column(skip_ref[...]), (heads, LANES))
    skip_pack = pack(jnp.transpose(jnp.concatenate([skip_col] * (LANES // heads), 0)), heads)

    def part(c):
        return pl.ds(pl.multiple_of(c * width, width), width)

    def role(d):
        lead = odd == d
        steps = jnp.where(d == 0, place, pairs - 1 - place)
        lead_row = jnp.broadcast_to(jnp.where(lead, 1, 0), (1, width)) == 1
        return lead, steps, lead_row

    def p_copy(d, c):
        return pltpu.make_async_remote_copy(
            src_ref=p_out.at[d, c],
            dst_ref=p_in.at[d, c],
            send_sem=p_send.at[d, c],
            recv_sem=p_recv.at[d, c],
            device_id={"seq": lax.rem(me + 2 - 4 * d + n_seq, n_seq)},
            device_id_type=MESH,
        )

    def m_copy(d, c):
        return pltpu.make_async_remote_copy(
            src_ref=m_out.at[d, c],
            dst_ref=entry.at[d, c],
            send_sem=m_send.at[d, c],
            recv_sem=m_recv.at[d, c],
            device_id={"seq": partner},
            device_id_type=MESH,
        )

    def l_copy(d, c):
        return pltpu.make_async_remote_copy(
            src_ref=local.at[d, c],
            dst_ref=other_local.at[d, c],
            send_sem=l_send.at[d, c],
            recv_sem=l_recv.at[d, c],
            device_id={"seq": partner},
            device_id_type=MESH,
        )

    half = chunks // 2
    round_about = pairs >= 4
    at_end = jnp.logical_or(place == 0, place == pairs - 1)
    by_end = jnp.logical_or(place == 1, place == pairs - 2)
    upper_half = jnp.where(place >= pairs // 2, 1, 0)
    outward = 4 * upper_half - 2

    def r_copy(leg, k):
        src, dst, target = [
            (m_out.at[upper_half, k + odd * half], relay.at[0, k], me + outward),
            (relay.at[0, k], relay.at[1, k], partner),
            (relay.at[1, k], entry.at[upper_half, k + (1 - odd) * half], me - outward),
        ][leg]
        return pltpu.make_async_remote_copy(
            src_ref=src,
            dst_ref=dst,
            send_sem=r_send.at[leg, k],
            recv_sem=r_recv.at[leg, k],
            device_id={"seq": lax.rem(target + n_seq, n_seq)},
            device_id_type=MESH,
        )

    def rerouted(d, k):
        return jnp.logical_and(jnp.logical_and(by_end, d == upper_half), k < 2)

    blank = jnp.zeros((LANES, width), F32)

    def step(d, c):
        lead, steps, lead_row = role(d)
        cols = part(c)
        own = rows[0:1, cols]
        other = rows[1:2, cols]
        wanted = jnp.logical_or(jnp.logical_not(lead), steps < pairs - 1)

        @pl.when(wanted)
        def _():
            l_copy(d, c).wait_recv()

        @pl.when(jnp.logical_not(wanted))
        def _():
            other_local[d, c] = blank

        @pl.when(steps > 0)
        def _():
            p_copy(d, c).wait_recv()

        @pl.when(steps == 0)
        def _():
            p_in[d, c] = blank

        before = p_in[d, c]
        here = local[d, c]
        there = other_local[d, c]

        @pl.when(steps < pairs - 1)
        def _():
            p_out[d, c] = own * other * before + jnp.where(
                lead_row, other * here + there, own * there + here
            )
            p_copy(d, c).start()

        m_out[d, c] = jnp.where(lead_row, own * before + here, before)

        k = c - odd * half
        sent = jnp.logical_or(lead, steps > 0)
        if round_about:
            aside = rerouted(d, k)

            @pl.when(aside)
            def _():
                r_copy(0, k).start()

            sent = jnp.logical_and(sent, jnp.logical_not(aside))

        @pl.when(sent)
        def _():
            m_copy(d, c).start()

        entry[d, c] = jnp.where(lead_row, before, other * before + there)

    def prepare(i, carry):
        c = lax.rem(i + (1 - odd) * half, chunks)
        cols = part(c)
        spread_c = spread[:, cols]
        e_c = dot(e_pack, spread_c)
        to_c = dot(to_pack, spread_c)
        e_wide[:, cols] = e_c
        to_wide[:, cols] = to_c
        x_c = x_ref[:, cols].astype(F32)
        g_c = g_ref[:, cols].astype(F32)
        sc = (x_c * to_c).astype(BF16)
        dv_c = (g_c * e_c).astype(BF16)
        scaled[:, cols] = sc
        dv[:, cols] = dv_c
        local[0, c] = dot(bt[...], sc)
        local[1, c] = dot(ct[...], dv_c)
        rows[:, cols] = jnp.zeros((8, width), F32)
        rows[0:1, cols] = e_c[span - 1 :, :]
        rows[2:3, cols] = dot(skip_pack[0:16], spread_c)[0:1]
        rows[4:5, cols] = jnp.sum(x_c * g_c, 0, keepdims=True)

        for d in range(2):
            lead, steps, _ = role(d)
            wanted = jnp.logical_or(lead, steps < pairs - 1)

            @pl.when(jnp.logical_and(i < half, wanted))
            def _():
                l_copy(d, c).start()

        return carry

    lax.fori_loop(0, chunks, prepare, 0)
    cb_ref[...] = dot(c_ref[...], b_ref[...], 1, 1)
    dcb[...] = jnp.zeros_like(dcb)
    sums[...] = jnp.zeros_like(sums)
    dcum[...] = jnp.zeros_like(dcum)
    gain_copy.wait()
    gain_pack = pack(gain_in[...], heads)
    rows[1:2, :] = dot(gain_pack, spread[...])[15:16, :]


    mid = span // 2
    low_part, high_part = slice(0, mid), slice(mid, span)
    lane = lax.broadcasted_iota(jnp.int32, (span, 2 * size), 1)
    lower = lax.broadcasted_iota(jnp.int32, (mid, mid), 0) >= lax.broadcasted_iota(
        jnp.int32, (mid, mid), 1
    )
    pick_row = lax.broadcasted_iota(jnp.int32, (LANES, mid), 0) & (heads - 1)

    def inner(j):
        cols = pl.ds(pl.multiple_of(j * 2 * size, 2 * size), 2 * size)
        x2 = x_ref[:, cols]
        g2 = g_ref[:, cols]
        y2, dx2 = [], []
        t00, t1 = 0.0, 0.0
        for i in range(2):
            h = 2 * j + i
            pick = jnp.where(pick_row == h, 1.0, 0.0).astype(BF16)
            at_t = dot(cum_pack[...], pick)
            row = cum_rows[pl.ds(h, 1), :]
            at_low, at_high = at_t[low_part], at_t[high_part]
            d00 = jnp.exp(jnp.where(lower, at_low - row[:, low_part], -1e30))
            d10 = jnp.exp(at_high - row[:, low_part])
            d11 = jnp.exp(jnp.where(lower, at_high - row[:, high_part], -1e30))
            d1 = jnp.concatenate([d10, d11], 1)
            w00 = (cb_ref[low_part, low_part] * d00).astype(BF16)
            w1 = (cb_ref[high_part, :] * d1).astype(BF16)
            y2.append(jnp.concatenate([dot(w00, x2[low_part]), dot(w1, x2)], 0))
            left = jnp.concatenate([w00, w1[:, low_part]], 0)
            dx2.append(
                jnp.concatenate([dot(left, g2, 0, 0), dot(w1[:, high_part], g2[high_part], 0, 0)], 0)
            )
            own_lanes = (lane < size) if i == 0 else (lane >= size)
            g_own = jnp.where(own_lanes, g2.astype(F32), 0.0).astype(BF16)
            t00 = t00 + dot(g_own[low_part], x2[low_part], 1, 1) * d00
            t1 = t1 + dot(g_own[high_part], x2, 1, 1) * d1
        dcb[low_part, low_part] += t00
        dcb[high_part, :] += t1
        y_acc[:, cols] = jnp.where(lane < size, y2[0], y2[1])
        dx_acc[:, cols] = jnp.where(lane < size, dx2[0], dx2[1])

    per_chunk = width // (2 * size)
    def middle(i, carry):
        if round_about:

            @pl.when(jnp.logical_and(at_end, jnp.logical_and(i >= 3, i < 5)))
            def _():
                r_copy(0, i - 3).wait_recv()
                r_copy(1, i - 3).start()

            @pl.when(jnp.logical_and(at_end, jnp.logical_and(i >= 6, i < 8)))
            def _():
                r_copy(1, i - 6).wait_recv()
                r_copy(2, i - 6).start()

        late = i // half
        step(upper_half + late - 2 * late * upper_half, lax.rem(i, half) + odd * half)
        for k in range(per_chunk):
            inner(i * per_chunk + k)
        return carry

    lax.fori_loop(0, chunks, middle, 0)

    dcb_low = dcb[...]
    dc_acc[...] = dot(dcb_low.astype(BF16), b_ref[...])
    db_acc[...] = dot(jnp.transpose(dcb_low).astype(BF16), c_ref[...])

    def finish(i, carry):
        c = lax.rem(i + odd * half, chunks)
        cols = part(c)
        for d in range(2):
            lead, steps, _ = role(d)
            nothing = jnp.logical_and(lead, steps == 0)

            @pl.when(jnp.logical_and(i >= half, nothing))
            def _():
                entry[d, c] = blank

            come = jnp.logical_and(i >= half, jnp.logical_not(nothing))
            if round_about:
                aside = jnp.logical_and(i >= half, rerouted(d, i - half))

                @pl.when(aside)
                def _():
                    r_copy(2, i - half).wait_recv()

                come = jnp.logical_and(come, jnp.logical_not(aside))

            @pl.when(come)
            def _():
                m_copy(d, c).wait_recv()

        state = entry[0, c]
        adj = entry[1, c]
        state_low = state.astype(BF16)
        adj_low = adj.astype(BF16)
        x_c = x_ref[:, cols].astype(F32)
        g_c = g_ref[:, cols].astype(F32)
        skip_c = rows[2:3, cols]
        y_c = y_acc[:, cols] + e_wide[:, cols] * dot(c_ref[...], state_low)
        y_ref[:, cols] = (y_c + skip_c * x_c).astype(BF16)
        dx_state = to_wide[:, cols] * dot(b_ref[...], adj_low)
        dx_c = dx_acc[:, cols] + dx_state
        gx_ref[:, cols] = (dx_c + skip_c * g_c).astype(BF16)
        dc_acc[...] += dot(dv[:, cols], state_low, 1, 1)
        db_acc[...] += dot(scaled[:, cols], adj_low, 1, 1)
        hi, low = halves(g_c * y_c - x_c * dx_c)
        sel = spread[0:heads, cols]
        dcum[...] += dot(sel, hi, 1, 1) + dot(sel, low, 1, 1)
        rows[3:4, cols] = jnp.sum(x_c * dx_state, 0, keepdims=True) + rows[0:1, cols] * jnp.sum(
            state * adj, 0, keepdims=True
        )
        hi, low = halves(jnp.concatenate([rows[:, cols], jnp.zeros((8, width), F32)], 0))
        sums[...] += dot(sel, hi, 1, 1) + dot(sel, low, 1, 1)
        return carry

    lax.fori_loop(0, chunks, finish, 0)

    per_head = sums[...]
    last = per_head[:, 3:4]
    alog = jnp.sum(dcum[...] * cum_rows[0:heads, :], 1, keepdims=True)
    alog_row = as_row(alog + last * cum_rows[0:heads, span - 1 : span])
    red_seq[me] = jnp.zeros((8, LANES), F32)
    red_seq[me, 0:1, 0:heads] = alog_row
    red_seq[me, 1:2, 0:heads] = as_row(per_head[:, 4:5])

    def share(axis, here, count, buf, send, recv, between):
        def copy(target, slot, o):
            return pltpu.make_async_remote_copy(
                src_ref=buf.at[here],
                dst_ref=buf.at[slot],
                send_sem=send.at[o],
                recv_sem=recv.at[slot],
                device_id={axis: target},
                device_id_type=MESH,
            )

        def go(o, carry):
            copy(lax.rem(here + o, count), here, o).start()
            return carry

        def come(o, carry):
            source = lax.rem(here + o, count)
            copy(source, source, o).wait_recv()
            copy(source, here, o).wait_send()
            return carry

        lax.fori_loop(1, count, go, 0)
        between()
        lax.fori_loop(1, count, come, 0)
        return jnp.sum(buf[...], 0)

    stores = [
        pltpu.make_async_copy(src, dst, store_sem.at[i])
        for i, (src, dst) in enumerate(
            [
                (y_ref, y_hbm),
                (gx_ref, gx_hbm),
                (gb_ref, gb_hbm),
                (gc_ref, gc_hbm),
                (gdt_ref, gdt_hbm),
            ]
        )
    ]

    def meanwhile():
        stores[0].start()
        stores[1].start()
        gc_ref[...] = dc_acc[...].astype(BF16)
        gb_ref[...] = db_acc[...].astype(BF16)
        stores[2].start()
        stores[3].start()
        lower_f = jnp.where(t_row >= t_col, 1.0, 0.0).astype(F32)
        dla = dot(dcum[...], lower_f, precision=lax.Precision.HIGHEST) + last
        gdt_ref[...] = -rate * dla
        stores[4].start()

    red_dp[mine] = share("seq", me, n_seq, red_seq, rs_send, rs_recv, meanwhile)
    total = share("dp", mine, n_dp, red_dp, rd_send, rd_recv, lambda: None)
    ga_ref[...] = total[0:1, 0:heads]
    gs_ref[...] = total[1:2, 0:heads]

    def drain(i, carry):
        c = i + odd * half
        away = i + (1 - odd) * half
        for d in range(2):
            lead, steps, _ = role(d)

            @pl.when(steps < pairs - 1)
            def _():
                p_copy(d, c).wait_send()

            sent = jnp.logical_or(lead, steps > 0)
            if round_about:
                aside = rerouted(d, i)

                @pl.when(aside)
                def _():
                    r_copy(0, i).wait_send()

                sent = jnp.logical_and(sent, jnp.logical_not(aside))

            @pl.when(sent)
            def _():
                m_copy(d, c).wait_send()

            @pl.when(jnp.logical_or(lead, steps < pairs - 1))
            def _():
                l_copy(d, away).wait_send()

        return carry

    lax.fori_loop(0, half, drain, 0)
    if round_about:

        @pl.when(at_end)
        def _():
            for k in range(2):
                r_copy(1, k).wait_send()
                r_copy(2, k).wait_send()

    for move in stores:
        move.wait()


def write_out(count, pieces, *refs):
    held = refs[2 * count : 3 * count]
    load, store = refs[3 * count :]
    moves = []
    for i in range(count):
        cuts = pieces if i < 2 else 1
        size = held[i].shape[0] // cuts
        for k in range(cuts):
            at = pl.ds(k * size, size)
            n = len(moves)
            moves.append(
                (
                    pltpu.make_async_copy(refs[i].at[at], held[i].at[at], load.at[n]),
                    pltpu.make_async_copy(held[i].at[at], refs[count + i].at[at], store.at[n]),
                )
            )
    for first, _ in moves:
        first.start()
    for first, second in moves:
        first.wait()
        second.start()
    for _, second in moves:
        second.wait()


def shards(n_seq, n_dp, x_in, b_in, c_in, dt, a_log, skip, cotangent):
    _, span, feat = x_in.shape
    state_dim = b_in.shape[2]
    heads = a_log.shape[0]
    width = 256
    chunks = feat // width
    blocks = (2, chunks, state_dim, width)
    vmem = pl.BlockSpec(memory_space=pltpu.VMEM)
    hbm = pl.BlockSpec(memory_space=pltpu.HBM)
    dma = pltpu.SemaphoreType.DMA
    wide = pltpu.VMEM((span, feat), F32)
    wide_low = pltpu.VMEM((span, feat), BF16)
    outs = pl.pallas_call(
        functools.partial(kernel, n_seq, n_dp, width),
        out_shape=(
            jax.ShapeDtypeStruct((span, feat), BF16),
            jax.ShapeDtypeStruct((span, feat), BF16),
            jax.ShapeDtypeStruct((span, state_dim), BF16),
            jax.ShapeDtypeStruct((span, state_dim), BF16),
            jax.ShapeDtypeStruct((heads, span), F32),
            jax.ShapeDtypeStruct((1, heads), F32),
            jax.ShapeDtypeStruct((1, heads), F32),
        ),
        in_specs=[hbm] * 7,
        out_specs=(hbm,) * 5 + (vmem,) * 2,
        scratch_shapes=[
            wide_low,
            wide_low,
            pltpu.VMEM((span, state_dim), BF16),
            pltpu.VMEM((span, state_dim), BF16),
            pltpu.VMEM((heads, span), F32),
            wide_low,
            pltpu.VMEM((span, state_dim), BF16),
            pltpu.VMEM((span, state_dim), BF16),
            pltpu.VMEM((heads, span), F32),
            pltpu.VMEM((1, heads), F32),
            pltpu.VMEM((1, heads), F32),
            wide_low,
            pltpu.VMEM((LANES, feat), BF16),
            pltpu.VMEM((LANES, span), F32),
            pltpu.VMEM((span, LANES), BF16),
            wide,
            wide,
            wide_low,
            wide_low,
            pltpu.VMEM((state_dim, span), BF16),
            pltpu.VMEM((state_dim, span), BF16),
            pltpu.VMEM(blocks, F32),
            pltpu.VMEM(blocks, F32),
            pltpu.VMEM(blocks, F32),
            pltpu.VMEM(blocks, F32),
            pltpu.VMEM(blocks, F32),
            pltpu.VMEM(blocks, F32),
            pltpu.VMEM((2, 2, state_dim, width), F32),
            pltpu.VMEM((8, feat), F32),
            wide,
            wide,
            pltpu.VMEM((span, span), F32),
            pltpu.VMEM((span, span), F32),
            pltpu.VMEM((span, state_dim), F32),
            pltpu.VMEM((span, state_dim), F32),
            pltpu.VMEM((heads, span), F32),
            pltpu.VMEM((heads, 16), F32),
            pltpu.VMEM((16, LANES), F32),
            pltpu.VMEM((16, LANES), F32),
            pltpu.VMEM((n_seq, 8, LANES), F32),
            pltpu.VMEM((n_dp, 8, LANES), F32),
            dma((2, chunks)),
            dma((2, chunks)),
            dma((2, chunks)),
            dma((2, chunks)),
            dma((2, chunks)),
            dma((2, chunks)),
            dma((3, 2)),
            dma((3, 2)),
            dma((2,)),
            dma((7,)),
            dma((5,)),
            dma((n_seq,)),
            dma((n_seq,)),
            dma((n_dp,)),
            dma((n_dp,)),
        ],
        compiler_params=pltpu.CompilerParams(
            collective_id=0, has_side_effects=True, vmem_limit_bytes=VMEM_BYTES
        ),
    )(x_in[0], b_in[0], c_in[0], dt[0], a_log[None], skip[None], cotangent[0])
    y, gx, gb, gc, gdt, ga, gs = pl.pallas_call(
        functools.partial(write_out, len(outs), 4),
        out_shape=tuple(jax.ShapeDtypeStruct(o.shape, o.dtype) for o in outs),
        in_specs=[hbm] * len(outs),
        out_specs=(hbm,) * len(outs),
        scratch_shapes=[pltpu.VMEM(o.shape, o.dtype) for o in outs]
        + [dma((len(outs) + 6,)), dma((len(outs) + 6,))],
        compiler_params=pltpu.CompilerParams(vmem_limit_bytes=VMEM_BYTES),
    )(*outs)
    return (y[None], gx[None], gb[None], gc[None], gdt[None], ga[0], gs[0])


def solution(mesh):
    tokens = P("dp", "seq", None)
    steps = P("dp", None, "seq")
    return jax.shard_map(
        functools.partial(shards, mesh.shape["seq"], mesh.shape["dp"]),
        mesh=mesh,
        in_specs=(tokens, tokens, tokens, steps, P(), P(), tokens),
        out_specs=(tokens, tokens, tokens, tokens, steps, P(), P()),
        check_vma=False,
    )
```

```python
import functools

import jax
import jax.numpy as jnp
from jax import lax
from jax.experimental import pallas as pl
from jax.experimental.pallas import tpu as pltpu
from jax.sharding import PartitionSpec as P

F32 = jnp.float32
BF16 = jnp.bfloat16
MESH = pl.DeviceIdType.MESH
LANES = 128
VMEM_BYTES = 62 * 1024 * 1024


def dot(a, b, ca=1, cb=0, precision=None):
    return lax.dot_general(
        a, b, (((ca,), (cb,)), ((), ())), preferred_element_type=F32, precision=precision
    )


def pack(v, heads):
    lane = lax.broadcasted_iota(jnp.int32, v.shape, 1)
    hi = v.astype(BF16).astype(F32)
    rest = v - hi
    mid = rest.astype(BF16).astype(F32)
    low = rest - mid
    out = jnp.where(lane < heads, hi, jnp.where(lane < 2 * heads, mid, low))
    return jnp.where(lane < 3 * heads, out, 0.0).astype(BF16)


def halves(v):
    hi = v.astype(BF16)
    return hi, (v - hi.astype(F32)).astype(BF16)


def kernel(
    n_seq,
    n_dp,
    width,
    x_hbm,
    b_hbm,
    c_hbm,
    dt_hbm,
    alog_hbm,
    skip_hbm,
    g_hbm,
    y_hbm,
    gx_hbm,
    gb_hbm,
    gc_hbm,
    gdt_hbm,
    ga_ref,
    gs_ref,
    y_ref,
    gx_ref,
    gb_ref,
    gc_ref,
    gdt_ref,
    x_ref,
    b_ref,
    c_ref,
    dt_ref,
    alog_ref,
    skip_ref,
    g_ref,
    spread,
    cum_rows,
    cum_pack,
    e_wide,
    to_wide,
    scaled,
    dv,
    bt,
    ct,
    local,
    p_in,
    p_out,
    other_local,
    entry,
    m_out,
    relay,
    rows,
    y_acc,
    dx_acc,
    cb_ref,
    dcb,
    dc_acc,
    db_acc,
    dcum,
    sums,
    gain_own,
    gain_in,
    red_seq,
    red_dp,
    p_send,
    p_recv,
    m_send,
    m_recv,
    l_send,
    l_recv,
    r_send,
    r_recv,
    g_sem,
    load_sem,
    store_sem,
    rs_send,
    rs_recv,
    rd_send,
    rd_recv,
):
    heads, span = dt_ref.shape
    feat = x_ref.shape[1]
    size = feat // heads
    chunks = feat // width
    pairs = n_seq // 2
    me = lax.axis_index("seq")
    mine = lax.axis_index("dp")
    place = me // 2
    odd = lax.rem(me, 2)
    partner = me + 1 - 2 * odd

    moves = [
        pltpu.make_async_copy(src, dst, load_sem.at[i])
        for i, (src, dst) in enumerate(
            [
                (dt_hbm, dt_ref),
                (alog_hbm, alog_ref),
                (skip_hbm, skip_ref),
                (b_hbm, b_ref),
                (c_hbm, c_ref),
                (x_hbm, x_ref),
                (g_hbm, g_ref),
            ]
        )
    ]
    for move in moves:
        move.start()
    barrier = pltpu.get_barrier_semaphore()

    def greet_seq(o, carry):
        pl.semaphore_signal(
            barrier, inc=1, device_id={"seq": lax.rem(me + o, n_seq)}, device_id_type=MESH
        )
        return carry

    def greet_dp(o, carry):
        pl.semaphore_signal(
            barrier, inc=1, device_id={"dp": lax.rem(mine + o, n_dp)}, device_id_type=MESH
        )
        return carry

    lax.fori_loop(1, n_seq, greet_seq, 0)
    lax.fori_loop(1, n_dp, greet_dp, 0)

    diag = lax.broadcasted_iota(jnp.int32, (heads, heads), 0) == lax.broadcasted_iota(
        jnp.int32, (heads, heads), 1
    )

    def column(row):
        return jnp.sum(jnp.where(diag, jnp.broadcast_to(row, (heads, heads)), 0.0), 1, keepdims=True)

    def as_row(col):
        return jnp.sum(jnp.where(diag, jnp.broadcast_to(col, (heads, heads)), 0.0), 0, keepdims=True)

    spread_row = lax.broadcasted_iota(jnp.int32, spread.shape, 0) & (heads - 1)
    spread_col = lax.shift_right_logical(
        lax.broadcasted_iota(jnp.int32, spread.shape, 1), size.bit_length() - 1
    )
    spread[...] = jnp.where(spread_row == spread_col, 1.0, 0.0).astype(BF16)
    for move in moves[:3]:
        move.wait()
    rate = jnp.exp(column(alog_ref[...]))
    la = -rate * dt_ref[...]
    t_row = lax.broadcasted_iota(jnp.int32, (span, span), 0)
    t_col = lax.broadcasted_iota(jnp.int32, (span, span), 1)
    upper = jnp.where(t_row <= t_col, 1.0, 0.0).astype(F32)
    cum = dot(jnp.concatenate([la] * (LANES // heads), 0), upper, precision=lax.Precision.HIGHEST)
    cum_rows[...] = cum
    cum_t = jnp.transpose(cum)
    cum_pack[...] = pack(cum_t, heads)
    e_t = jnp.exp(cum_t)
    gain_own[...] = e_t[span - 16 :, :]
    pl.semaphore_wait(barrier, n_seq - 1 + n_dp - 1)
    gain_copy = pltpu.make_async_remote_copy(
        src_ref=gain_own,
        dst_ref=gain_in,
        send_sem=g_sem.at[0],
        recv_sem=g_sem.at[1],
        device_id={"seq": partner},
        device_id_type=MESH,
    )
    gain_copy.start()

    e_pack = pack(e_t, heads)
    to_pack = pack(jnp.exp(cum_t[span - 1 :, :] - cum_t), heads)
    for move in moves[3:]:
        move.wait()
    bt[...] = jnp.transpose(b_ref[...].astype(F32)).astype(BF16)
    ct[...] = jnp.transpose(c_ref[...].astype(F32)).astype(BF16)
    skip_col = jnp.broadcast_to(column(skip_ref[...]), (heads, LANES))
    skip_pack = pack(jnp.transpose(jnp.concatenate([skip_col] * (LANES // heads), 0)), heads)

    def part(c):
        return pl.ds(pl.multiple_of(c * width, width), width)

    def role(d):
        lead = odd == d
        steps = jnp.where(d == 0, place, pairs - 1 - place)
        lead_row = jnp.broadcast_to(jnp.where(lead, 1, 0), (1, width)) == 1
        return lead, steps, lead_row

    def p_copy(d, c):
        return pltpu.make_async_remote_copy(
            src_ref=p_out.at[d, c],
            dst_ref=p_in.at[d, c],
            send_sem=p_send.at[d, c],
            recv_sem=p_recv.at[d, c],
            device_id={"seq": lax.rem(me + 2 - 4 * d + n_seq, n_seq)},
            device_id_type=MESH,
        )

    def m_copy(d, c):
        return pltpu.make_async_remote_copy(
            src_ref=m_out.at[d, c],
            dst_ref=entry.at[d, c],
            send_sem=m_send.at[d, c],
            recv_sem=m_recv.at[d, c],
            device_id={"seq": partner},
            device_id_type=MESH,
        )

    def l_copy(d, c):
        return pltpu.make_async_remote_copy(
            src_ref=local.at[d, c],
            dst_ref=other_local.at[d, c],
            send_sem=l_send.at[d, c],
            recv_sem=l_recv.at[d, c],
            device_id={"seq": partner},
            device_id_type=MESH,
        )

    half = chunks // 2
    round_about = pairs >= 4
    at_end = jnp.logical_or(place == 0, place == pairs - 1)
    by_end = jnp.logical_or(place == 1, place == pairs - 2)
    upper_half = jnp.where(place >= pairs // 2, 1, 0)
    outward = 4 * upper_half - 2

    def r_copy(leg, k):
        src, dst, target = [
            (m_out.at[upper_half, k + odd * half], relay.at[0, k], me + outward),
            (relay.at[0, k], relay.at[1, k], partner),
            (relay.at[1, k], entry.at[upper_half, k + (1 - odd) * half], me - outward),
        ][leg]
        return pltpu.make_async_remote_copy(
            src_ref=src,
            dst_ref=dst,
            send_sem=r_send.at[leg, k],
            recv_sem=r_recv.at[leg, k],
            device_id={"seq": lax.rem(target + n_seq, n_seq)},
            device_id_type=MESH,
        )

    def rerouted(d, k):
        return jnp.logical_and(jnp.logical_and(by_end, d == upper_half), k < 2)

    blank = jnp.zeros((LANES, width), F32)

    def step(d, c):
        lead, steps, lead_row = role(d)
        cols = part(c)
        own = rows[0:1, cols]
        other = rows[1:2, cols]
        wanted = jnp.logical_or(jnp.logical_not(lead), steps < pairs - 1)

        @pl.when(wanted)
        def _():
            l_copy(d, c).wait_recv()

        @pl.when(jnp.logical_not(wanted))
        def _():
            other_local[d, c] = blank

        @pl.when(steps > 0)
        def _():
            p_copy(d, c).wait_recv()

        @pl.when(steps == 0)
        def _():
            p_in[d, c] = blank

        before = p_in[d, c]
        here = local[d, c]
        there = other_local[d, c]

        @pl.when(steps < pairs - 1)
        def _():
            p_out[d, c] = own * other * before + jnp.where(
                lead_row, other * here + there, own * there + here
            )
            p_copy(d, c).start()

        m_out[d, c] = jnp.where(lead_row, own * before + here, before)

        k = c - odd * half
        sent = jnp.logical_or(lead, steps > 0)
        if round_about:
            aside = rerouted(d, k)

            @pl.when(aside)
            def _():
                r_copy(0, k).start()

            sent = jnp.logical_and(sent, jnp.logical_not(aside))

        @pl.when(sent)
        def _():
            m_copy(d, c).start()

        entry[d, c] = jnp.where(lead_row, before, other * before + there)

    def prepare(i, carry):
        c = lax.rem(i + (1 - odd) * half, chunks)
        cols = part(c)
        spread_c = spread[:, cols]
        e_c = dot(e_pack, spread_c)
        to_c = dot(to_pack, spread_c)
        e_wide[:, cols] = e_c
        to_wide[:, cols] = to_c
        x_c = x_ref[:, cols].astype(F32)
        g_c = g_ref[:, cols].astype(F32)
        sc = (x_c * to_c).astype(BF16)
        dv_c = (g_c * e_c).astype(BF16)
        scaled[:, cols] = sc
        dv[:, cols] = dv_c
        local[0, c] = dot(bt[...], sc)
        local[1, c] = dot(ct[...], dv_c)
        rows[:, cols] = jnp.zeros((8, width), F32)
        rows[0:1, cols] = e_c[span - 1 :, :]
        rows[2:3, cols] = dot(skip_pack[0:16], spread_c)[0:1]
        rows[4:5, cols] = jnp.sum(x_c * g_c, 0, keepdims=True)

        for d in range(2):
            lead, steps, _ = role(d)
            wanted = jnp.logical_or(lead, steps < pairs - 1)

            @pl.when(jnp.logical_and(i < half, wanted))
            def _():
                l_copy(d, c).start()

        return carry

    lax.fori_loop(0, chunks, prepare, 0)
    cb_ref[...] = dot(c_ref[...], b_ref[...], 1, 1)
    dcb[...] = jnp.zeros_like(dcb)
    sums[...] = jnp.zeros_like(sums)
    dcum[...] = jnp.zeros_like(dcum)
    gain_copy.wait()
    gain_pack = pack(gain_in[...], heads)
    rows[1:2, :] = dot(gain_pack, spread[...])[15:16, :]


    mid = span // 2
    low_part, high_part = slice(0, mid), slice(mid, span)
    lane = lax.broadcasted_iota(jnp.int32, (span, 2 * size), 1)
    lower = lax.broadcasted_iota(jnp.int32, (mid, mid), 0) >= lax.broadcasted_iota(
        jnp.int32, (mid, mid), 1
    )
    pick_row = lax.broadcasted_iota(jnp.int32, (LANES, mid), 0) & (heads - 1)

    def inner(j):
        cols = pl.ds(pl.multiple_of(j * 2 * size, 2 * size), 2 * size)
        x2 = x_ref[:, cols]
        g2 = g_ref[:, cols]
        y2, dx2 = [], []
        t00, t1 = 0.0, 0.0
        for i in range(2):
            h = 2 * j + i
            pick = jnp.where(pick_row == h, 1.0, 0.0).astype(BF16)
            at_t = dot(cum_pack[...], pick)
            row = cum_rows[pl.ds(h, 1), :]
            at_low, at_high = at_t[low_part], at_t[high_part]
            d00 = jnp.exp(jnp.where(lower, at_low - row[:, low_part], -1e30))
            d10 = jnp.exp(at_high - row[:, low_part])
            d11 = jnp.exp(jnp.where(lower, at_high - row[:, high_part], -1e30))
            d1 = jnp.concatenate([d10, d11], 1)
            w00 = (cb_ref[low_part, low_part] * d00).astype(BF16)
            w1 = (cb_ref[high_part, :] * d1).astype(BF16)
            y2.append(jnp.concatenate([dot(w00, x2[low_part]), dot(w1, x2)], 0))
            left = jnp.concatenate([w00, w1[:, low_part]], 0)
            dx2.append(
                jnp.concatenate([dot(left, g2, 0, 0), dot(w1[:, high_part], g2[high_part], 0, 0)], 0)
            )
            own_lanes = (lane < size) if i == 0 else (lane >= size)
            g_own = jnp.where(own_lanes, g2.astype(F32), 0.0).astype(BF16)
            t00 = t00 + dot(g_own[low_part], x2[low_part], 1, 1) * d00
            t1 = t1 + dot(g_own[high_part], x2, 1, 1) * d1
        dcb[low_part, low_part] += t00
        dcb[high_part, :] += t1
        y_acc[:, cols] = jnp.where(lane < size, y2[0], y2[1])
        dx_acc[:, cols] = jnp.where(lane < size, dx2[0], dx2[1])

    per_chunk = width // (2 * size)
    def middle(i):
        if round_about:

            @pl.when(jnp.logical_and(at_end, jnp.logical_and(i >= 3, i < 5)))
            def _():
                r_copy(0, i - 3).wait_recv()
                r_copy(1, i - 3).start()

            @pl.when(jnp.logical_and(at_end, jnp.logical_and(i >= 6, i < 8)))
            def _():
                r_copy(1, i - 6).wait_recv()
                r_copy(2, i - 6).start()

        late = i // half
        step(upper_half + late - 2 * late * upper_half, lax.rem(i, half) + odd * half)

    def early(i, carry):
        middle(i)
        for k in range(2 * per_chunk):
            inner(2 * i * per_chunk + k)
        return carry

    lax.fori_loop(0, half, early, 0)

    dcb_low = dcb[...]
    dc_acc[...] = dot(dcb_low.astype(BF16), b_ref[...])
    db_acc[...] = dot(jnp.transpose(dcb_low).astype(BF16), c_ref[...])

    def finish(i, carry):
        c = lax.rem(i + odd * half, chunks)
        cols = part(c)
        for d in range(2):
            lead, steps, _ = role(d)
            nothing = jnp.logical_and(lead, steps == 0)

            @pl.when(jnp.logical_and(i >= half, nothing))
            def _():
                entry[d, c] = blank

            come = jnp.logical_and(i >= half, jnp.logical_not(nothing))
            if round_about:
                aside = jnp.logical_and(i >= half, rerouted(d, i - half))

                @pl.when(aside)
                def _():
                    r_copy(2, i - half).wait_recv()

                come = jnp.logical_and(come, jnp.logical_not(aside))

            @pl.when(come)
            def _():
                m_copy(d, c).wait_recv()

        state = entry[0, c]
        adj = entry[1, c]
        state_low = state.astype(BF16)
        adj_low = adj.astype(BF16)
        x_c = x_ref[:, cols].astype(F32)
        g_c = g_ref[:, cols].astype(F32)
        skip_c = rows[2:3, cols]
        y_c = y_acc[:, cols] + e_wide[:, cols] * dot(c_ref[...], state_low)
        y_ref[:, cols] = (y_c + skip_c * x_c).astype(BF16)
        dx_state = to_wide[:, cols] * dot(b_ref[...], adj_low)
        dx_c = dx_acc[:, cols] + dx_state
        gx_ref[:, cols] = (dx_c + skip_c * g_c).astype(BF16)
        dc_acc[...] += dot(dv[:, cols], state_low, 1, 1)
        db_acc[...] += dot(scaled[:, cols], adj_low, 1, 1)
        hi, low = halves(g_c * y_c - x_c * dx_c)
        sel = spread[0:heads, cols]
        dcum[...] += dot(sel, hi, 1, 1) + dot(sel, low, 1, 1)
        rows[3:4, cols] = jnp.sum(x_c * dx_state, 0, keepdims=True) + rows[0:1, cols] * jnp.sum(
            state * adj, 0, keepdims=True
        )
        hi, low = halves(jnp.concatenate([rows[:, cols], jnp.zeros((8, width), F32)], 0))
        sums[...] += dot(sel, hi, 1, 1) + dot(sel, low, 1, 1)
        return carry

    def later(i, carry):
        middle(i)
        return finish(i - half, carry)

    lax.fori_loop(half, chunks, later, 0)
    lax.fori_loop(half, chunks, finish, 0)

    per_head = sums[...]
    last = per_head[:, 3:4]
    alog = jnp.sum(dcum[...] * cum_rows[0:heads, :], 1, keepdims=True)
    alog_row = as_row(alog + last * cum_rows[0:heads, span - 1 : span])
    red_seq[me] = jnp.zeros((8, LANES), F32)
    red_seq[me, 0:1, 0:heads] = alog_row
    red_seq[me, 1:2, 0:heads] = as_row(per_head[:, 4:5])

    def share(axis, here, count, buf, send, recv, between):
        def copy(target, slot, o):
            return pltpu.make_async_remote_copy(
                src_ref=buf.at[here],
                dst_ref=buf.at[slot],
                send_sem=send.at[o],
                recv_sem=recv.at[slot],
                device_id={axis: target},
                device_id_type=MESH,
            )

        def go(o, carry):
            copy(lax.rem(here + o, count), here, o).start()
            return carry

        def come(o, carry):
            source = lax.rem(here + o, count)
            copy(source, source, o).wait_recv()
            copy(source, here, o).wait_send()
            return carry

        lax.fori_loop(1, count, go, 0)
        between()
        lax.fori_loop(1, count, come, 0)
        return jnp.sum(buf[...], 0)

    stores = [
        pltpu.make_async_copy(src, dst, store_sem.at[i])
        for i, (src, dst) in enumerate(
            [
                (y_ref, y_hbm),
                (gx_ref, gx_hbm),
                (gb_ref, gb_hbm),
                (gc_ref, gc_hbm),
                (gdt_ref, gdt_hbm),
            ]
        )
    ]

    def meanwhile():
        stores[0].start()
        stores[1].start()
        gc_ref[...] = dc_acc[...].astype(BF16)
        gb_ref[...] = db_acc[...].astype(BF16)
        stores[2].start()
        stores[3].start()
        lower_f = jnp.where(t_row >= t_col, 1.0, 0.0).astype(F32)
        dla = dot(dcum[...], lower_f, precision=lax.Precision.HIGHEST) + last
        gdt_ref[...] = -rate * dla
        stores[4].start()

    red_dp[mine] = share("seq", me, n_seq, red_seq, rs_send, rs_recv, meanwhile)
    total = share("dp", mine, n_dp, red_dp, rd_send, rd_recv, lambda: None)
    ga_ref[...] = total[0:1, 0:heads]
    gs_ref[...] = total[1:2, 0:heads]

    def drain(i, carry):
        c = i + odd * half
        away = i + (1 - odd) * half
        for d in range(2):
            lead, steps, _ = role(d)

            @pl.when(steps < pairs - 1)
            def _():
                p_copy(d, c).wait_send()

            sent = jnp.logical_or(lead, steps > 0)
            if round_about:
                aside = rerouted(d, i)

                @pl.when(aside)
                def _():
                    r_copy(0, i).wait_send()

                sent = jnp.logical_and(sent, jnp.logical_not(aside))

            @pl.when(sent)
            def _():
                m_copy(d, c).wait_send()

            @pl.when(jnp.logical_or(lead, steps < pairs - 1))
            def _():
                l_copy(d, away).wait_send()

        return carry

    lax.fori_loop(0, half, drain, 0)
    if round_about:

        @pl.when(at_end)
        def _():
            for k in range(2):
                r_copy(1, k).wait_send()
                r_copy(2, k).wait_send()

    for move in stores:
        move.wait()


def write_out(count, pieces, *refs):
    held = refs[2 * count : 3 * count]
    load, store = refs[3 * count :]
    moves = []
    for i in range(count):
        cuts = pieces if i < 2 else 1
        size = held[i].shape[0] // cuts
        for k in range(cuts):
            at = pl.ds(k * size, size)
            n = len(moves)
            moves.append(
                (
                    pltpu.make_async_copy(refs[i].at[at], held[i].at[at], load.at[n]),
                    pltpu.make_async_copy(held[i].at[at], refs[count + i].at[at], store.at[n]),
                )
            )
    for first, _ in moves:
        first.start()
    for first, second in moves:
        first.wait()
        second.start()
    for _, second in moves:
        second.wait()


def shards(n_seq, n_dp, x_in, b_in, c_in, dt, a_log, skip, cotangent):
    _, span, feat = x_in.shape
    state_dim = b_in.shape[2]
    heads = a_log.shape[0]
    width = 256
    chunks = feat // width
    blocks = (2, chunks, state_dim, width)
    vmem = pl.BlockSpec(memory_space=pltpu.VMEM)
    hbm = pl.BlockSpec(memory_space=pltpu.HBM)
    dma = pltpu.SemaphoreType.DMA
    wide = pltpu.VMEM((span, feat), F32)
    wide_low = pltpu.VMEM((span, feat), BF16)
    outs = pl.pallas_call(
        functools.partial(kernel, n_seq, n_dp, width),
        out_shape=(
            jax.ShapeDtypeStruct((span, feat), BF16),
            jax.ShapeDtypeStruct((span, feat), BF16),
            jax.ShapeDtypeStruct((span, state_dim), BF16),
            jax.ShapeDtypeStruct((span, state_dim), BF16),
            jax.ShapeDtypeStruct((heads, span), F32),
            jax.ShapeDtypeStruct((1, heads), F32),
            jax.ShapeDtypeStruct((1, heads), F32),
        ),
        in_specs=[hbm] * 7,
        out_specs=(hbm,) * 5 + (vmem,) * 2,
        scratch_shapes=[
            wide_low,
            wide_low,
            pltpu.VMEM((span, state_dim), BF16),
            pltpu.VMEM((span, state_dim), BF16),
            pltpu.VMEM((heads, span), F32),
            wide_low,
            pltpu.VMEM((span, state_dim), BF16),
            pltpu.VMEM((span, state_dim), BF16),
            pltpu.VMEM((heads, span), F32),
            pltpu.VMEM((1, heads), F32),
            pltpu.VMEM((1, heads), F32),
            wide_low,
            pltpu.VMEM((LANES, feat), BF16),
            pltpu.VMEM((LANES, span), F32),
            pltpu.VMEM((span, LANES), BF16),
            wide,
            wide,
            wide_low,
            wide_low,
            pltpu.VMEM((state_dim, span), BF16),
            pltpu.VMEM((state_dim, span), BF16),
            pltpu.VMEM(blocks, F32),
            pltpu.VMEM(blocks, F32),
            pltpu.VMEM(blocks, F32),
            pltpu.VMEM(blocks, F32),
            pltpu.VMEM(blocks, F32),
            pltpu.VMEM(blocks, F32),
            pltpu.VMEM((2, 2, state_dim, width), F32),
            pltpu.VMEM((8, feat), F32),
            wide,
            wide,
            pltpu.VMEM((span, span), F32),
            pltpu.VMEM((span, span), F32),
            pltpu.VMEM((span, state_dim), F32),
            pltpu.VMEM((span, state_dim), F32),
            pltpu.VMEM((heads, span), F32),
            pltpu.VMEM((heads, 16), F32),
            pltpu.VMEM((16, LANES), F32),
            pltpu.VMEM((16, LANES), F32),
            pltpu.VMEM((n_seq, 8, LANES), F32),
            pltpu.VMEM((n_dp, 8, LANES), F32),
            dma((2, chunks)),
            dma((2, chunks)),
            dma((2, chunks)),
            dma((2, chunks)),
            dma((2, chunks)),
            dma((2, chunks)),
            dma((3, 2)),
            dma((3, 2)),
            dma((2,)),
            dma((7,)),
            dma((5,)),
            dma((n_seq,)),
            dma((n_seq,)),
            dma((n_dp,)),
            dma((n_dp,)),
        ],
        compiler_params=pltpu.CompilerParams(
            collective_id=0, has_side_effects=True, vmem_limit_bytes=VMEM_BYTES
        ),
    )(x_in[0], b_in[0], c_in[0], dt[0], a_log[None], skip[None], cotangent[0])
    y, gx, gb, gc, gdt, ga, gs = pl.pallas_call(
        functools.partial(write_out, len(outs), 4),
        out_shape=tuple(jax.ShapeDtypeStruct(o.shape, o.dtype) for o in outs),
        in_specs=[hbm] * len(outs),
        out_specs=(hbm,) * len(outs),
        scratch_shapes=[pltpu.VMEM(o.shape, o.dtype) for o in outs]
        + [dma((len(outs) + 6,)), dma((len(outs) + 6,))],
        compiler_params=pltpu.CompilerParams(vmem_limit_bytes=VMEM_BYTES),
    )(*outs)
    return (y[None], gx[None], gb[None], gc[None], gdt[None], ga[0], gs[0])


def solution(mesh):
    tokens = P("dp", "seq", None)
    steps = P("dp", None, "seq")
    return jax.shard_map(
        functools.partial(shards, mesh.shape["seq"], mesh.shape["dp"]),
        mesh=mesh,
        in_specs=(tokens, tokens, tokens, steps, P(), P(), tokens),
        out_specs=(tokens, tokens, tokens, tokens, steps, P(), P()),
        check_vma=False,
    )
```
